128 devices in a mesh: group: 4 (over y), tensor: 32 (over x, z, core).
Axes of the slice: x: 4, y: 4, z: 4, core: 2. Of those that a mesh axis runs over, the one named last changes fastest.
Arguments:
- requests: bfloat16 [2048, 7168], P(('group', 'tensor')), parts along dimension 0, may hold values from -6 to 6
- counts: int32 [128], P('group'), parts along dimension 0, may hold values from 1 to 16, 256 in all
- gate_weight: bfloat16 [7168, 18432], P(None, 'tensor'), may hold values from -0.0625 to 0.0625
- up_weight: bfloat16 [7168, 18432], P(None, 'tensor'), may hold values from -0.0625 to 0.0625
- down_weight: bfloat16 [18432, 7168], P('tensor'), may hold values from -0.046875 to 0.046875
Outputs:
- finished: bfloat16 [2048, 7168], P(('group', 'tensor')), parts along dimension 0
The draws below stay inside these ranges and needn't reach their ends.
There are 4 independent parts, one for each index of `group`. The reference program is written for one: setup_inputs(seed, part) draws one part's arguments, and reference() takes and returns one part's arrays. A program takes and returns all parts, laid end to end along the dimension named above; an argument that names none is the same for every part. Nothing has to cross between parts.
Inputs may be any that keep to these rules, and one draw needn't show every extreme that they name: Each group's counts add up to 256, and in every group some replica holds exactly 16 requests.
All inputs are finite; a program needn't handle non-finite values.
Results may differ from the reference program's by a relative error of at most 0.0058.
Values may be sent and summed in bfloat16 or wider, within the bound.
A program may use at most 128 MiB of HBM per device.

```python
import math
import jax
import jax.numpy as jnp
import numpy as np
from jax import lax

D = 7168
FF = 18432
ROWS = 256
CAP = 16
N_TENSOR = 32


def steps_of(own_key, extent, split, low, largest):
    def one(axis_at, parts):
        heights = jax.random.uniform(jax.random.fold_in(jax.random.fold_in(own_key, 6), axis_at), (parts,), jnp.float32, low / len(split), largest / len(split))
        return jnp.repeat(jnp.exp(heights), extent[axis_at] // parts).reshape((-1,) + (1,) * (len(extent) - axis_at - 1))

    gain = one(*split[0])
    for cut in split[1:]:
        gain = gain * one(*cut)
    return gain


def split_up(count, total, limit, lean):
    loads = [(1 << 20) // math.isqrt(standing ** lean) + 1 for standing in range(2, count + 1)]
    spare, holding = total - limit - (count - 1), [1] * (count - 1)
    while spare > 0:
        free = [i for i in range(count - 1) if holding[i] < limit]
        pool, remaining = sum([loads[i] for i in free]), spare
        for i in free:
            more = min(limit - holding[i], max(1, remaining * loads[i] // pool), spare)
            holding[i] = holding[i] + more
            spare = spare - more
    return np.array([limit] + holding)


def uneven_parts(key, amount, total, reach, lean):
    if amount == 2:
        one = jax.random.randint(key, (), max(1, total - reach), min(reach, total - 1) + 1)
        return jnp.stack([one, total - one])
    sizes = jnp.asarray(split_up(amount, total, reach, lean), jnp.int32)
    twos = (amount - 1) // 2
    source_of, sink = sizes[1:1 + 2 * twos:2], sizes[2:2 + 2 * twos:2]
    room = jnp.minimum(source_of - 1, reach - sink)
    shifted = jax.random.randint(jax.random.fold_in(key, 1), (twos,), 0, 1 << 20) % (room + 1)
    sizes = sizes.at[1:1 + 2 * twos:2].set(source_of - shifted).at[2:2 + 2 * twos:2].set(sink + shifted)
    return sizes[jax.random.permutation(jax.random.fold_in(key, 2), amount)]


def noise(stream_key, dims, width, bound, shards=(), kind=jnp.bfloat16):
    factor_of = steps_of(stream_key, dims, shards, -0.22, 0.18) if shards else 1.0
    drawn = jax.random.normal(stream_key, dims, jnp.float32) * width * factor_of
    return jnp.minimum(jnp.maximum(drawn, -bound), bound).astype(kind)


def setup_inputs(seed: int = 0, part: int = 0) -> dict:
    arg_keys = jax.random.split(jax.random.key(seed), 6)
    part_splits = jax.random.split(jax.random.fold_in(arg_keys[5], part), 6)
    requests = noise(part_splits[0], (N_TENSOR * CAP, D), 1.0, 6.0, ((0, 32),))
    counts = uneven_parts(part_splits[1], N_TENSOR, ROWS, CAP, 2).astype(jnp.int32)
    gate_weight = noise(arg_keys[2], (D, FF), D ** -0.5, 0.0625, ((1, 32),))
    up_weight = noise(arg_keys[3], (D, FF), D ** -0.5, 0.0625, ((1, 32),))
    down_weight = noise(arg_keys[4], (FF, D), FF ** -0.5, 0.046875, ((0, 32),))
    return dict(requests=requests, counts=counts, gate_weight=gate_weight, up_weight=up_weight, down_weight=down_weight)


def reference(requests, counts, gate_weight, up_weight, down_weight):
    counts = counts.astype(jnp.int32)
    offsets = (jnp.cumsum(counts) - counts).astype(jnp.int32)
    row_ends = (offsets + counts).astype(jnp.int32)
    positions = jnp.arange(ROWS, dtype=jnp.int32)
    owners = jnp.sum((positions[:, None] >= row_ends[None, :]).astype(jnp.int32), axis=1).astype(jnp.int32)
    row_starts = offsets[owners]
    source = (owners * CAP + positions - row_starts).astype(jnp.int32)
    packed = jnp.take(requests, source, axis=0)
    block_width = FF // N_TENSOR

    def add_block(block_index, total_sum):
        first_col = (block_index * block_width).astype(jnp.int32)
        gate_block = lax.dynamic_slice_in_dim(gate_weight, first_col, block_width, 1)
        up_block = lax.dynamic_slice_in_dim(up_weight, first_col, block_width, 1)
        down_block = lax.dynamic_slice_in_dim(down_weight, first_col, block_width, 0)
        gate_sum = jnp.dot(packed, gate_block, preferred_element_type=jnp.float32)
        up_sum = jnp.dot(packed, up_block, preferred_element_type=jnp.float32)
        hidden = (jax.nn.silu(gate_sum) * up_sum).astype(jnp.bfloat16)
        partial_value = jnp.dot(hidden, down_block, preferred_element_type=jnp.float32).astype(jnp.bfloat16)
        partial_value = lax.optimization_barrier(partial_value)
        return total_sum + partial_value.astype(jnp.float32)

    summed = lax.fori_loop(0, N_TENSOR, add_block, jnp.zeros((ROWS, D), jnp.float32))
    rounded = summed.astype(jnp.bfloat16)
    slot_index = jnp.arange(CAP, dtype=jnp.int32)
    local_rows = (offsets[:, None] + slot_index[None, :]).astype(jnp.int32)
    in_use = slot_index[None, :] < counts[:, None]
    picked = jnp.take(rounded, jnp.clip(local_rows, 0, ROWS - 1).reshape(-1), axis=0).reshape(N_TENSOR, CAP, D)
    finished = jnp.where(in_use[:, :, None], picked, jnp.zeros_like(picked))
    return finished.reshape(N_TENSOR * CAP, D)
```

```python
import functools

import jax
import jax.numpy as jnp
from jax import lax
from jax.experimental import pallas as pl
from jax.experimental.pallas import tpu as pltpu
from jax.sharding import PartitionSpec as P

SIDE = 4
CHIPS = SIDE * SIDE
DEVICES = 2 * CHIPS
CAP = 16
ROWS = 256
LANES = 128
MESH = pl.DeviceIdType.MESH


def stream_widths(half):
    tile = 256 if half % 256 == 0 and half >= 1024 else 128
    tiles = half // tile
    first = (tiles + 3) // 4
    pair = tiles // 2
    return [first * tile, (pair - first) * tile] * 2


def kernel(
    req, counts, wg_hbm, wu_hbm, wd_hbm, out,
    wg, wu, wd, spread, spread2, pkt, rows_in, inbox, grid, gate, up, hidden,
    pout, pin, chip_sum, big_in, quad_sum, small_in, final, rows_out, pkt_back, inbox_back, offs,
    w_sem, a_send, a_recv, g_send, g_recv, r_send, r_recv, b_send, b_recv,
):
    features = req.shape[1]
    half = features // 2
    hb = half // LANES
    rp = inbox.shape[1]
    widths = stream_widths(half)
    starts = [sum(widths[:s]) for s in range(4)]

    me = lax.axis_index("tensor")
    core = lax.rem(me, 2)
    other = 1 - core
    chip = me // 2
    x = chip // SIDE
    z = lax.rem(chip, SIDE)

    def device(xx, zz, cc):
        return {"tensor": (xx * SIDE + zz) * 2 + cc}

    sibling = device(x, z, other)

    barrier = pltpu.get_barrier_semaphore()

    @pl.loop(1, DEVICES)
    def _(s):
        pl.semaphore_signal(
            barrier, inc=1, device_id={"tensor": lax.rem(me + s, DEVICES)}, device_id_type=MESH
        )

    loads = {}
    for turn, c in enumerate((core, other)):
        for s in range(4):
            rows = pl.ds(pl.multiple_of(c * half + starts[s], LANES), widths[s])
            pair = []
            for n, (src, dst) in enumerate(((wg_hbm, wg), (wu_hbm, wu))):
                copy = pltpu.make_async_copy(src.at[rows], dst.at[rows], w_sem.at[turn * 8 + s * 2 + n])
                copy.start()
                pair.append(copy)
            loads[turn, s] = pair
    wd_load = pltpu.make_async_copy(wd_hbm, wd, w_sem.at[16])
    wd_load.start()

    total = jnp.int32(0)
    ends = []
    for i in range(DEVICES):
        offs[i] = total
        total = total + counts[i]
        ends.append(total)
    my_off = offs[me]
    my_count = counts[me]

    spread[...] = jnp.zeros_like(spread)
    for h in range(2):
        for m in range(hb):
            block = req[:, (h * hb + m) * LANES : (h * hb + m + 1) * LANES]
            spread[pl.ds(h * rp + m, CAP, stride=2 * rp), :] = block.astype(jnp.float32)

    def row_for(p, off):
        return lax.rem(p - off + ROWS, CAP)

    for j in range(CAP):
        for h in range(2):
            at = (2 * j + h) * rp
            rows_in[j, h] = spread[at : at + rp, :].astype(jnp.bfloat16)
    for p in range(CHIPS):
        pkt[p] = rows_in[row_for(p, my_off)]
    inbox[me] = pkt[chip, core]

    pl.semaphore_wait(barrier, DEVICES - 1)

    def dispatch(s):
        t = lax.rem(me + s, DEVICES)
        return pltpu.make_async_remote_copy(
            src_ref=pkt.at[t // 2, lax.rem(t, 2)], dst_ref=inbox.at[me],
            send_sem=a_send.at[s], recv_sem=a_recv.at[me],
            device_id={"tensor": t}, device_id_type=MESH,
        )

    def dispatched(s):
        t = lax.rem(me + s, DEVICES)
        return pltpu.make_async_remote_copy(
            src_ref=pkt.at[0, 0], dst_ref=inbox.at[t],
            send_sem=a_send.at[s], recv_sem=a_recv.at[t],
            device_id={"tensor": t}, device_id_type=MESH,
        )

    @pl.loop(1, DEVICES)
    def _(s):
        dispatch(s).start()

    owners = []
    for k in range(ROWS // CHIPS):
        rank = chip + CHIPS * k
        owner = jnp.int32(0)
        for end in ends[:-1]:
            owner = owner + (end <= rank).astype(jnp.int32)
        owners.append(owner)

    @pl.loop(1, DEVICES)
    def _(s):
        dispatched(s).wait_recv()

    for k in range(ROWS // CHIPS):
        spread2[k * rp : (k + 1) * rp, :] = inbox[owners[k]].astype(jnp.float32)
    for m in range(hb):
        block = spread2[pl.ds(m, CAP, stride=rp), :].astype(jnp.bfloat16)
        grid[core, x, z, :, m * LANES : (m + 1) * LANES] = block

    def cols(s):
        return pl.ds(starts[s], widths[s])

    def block_of(s, small, big):
        xx, zz = (small, big) if s < 2 else (big, small)
        return grid.at[core, xx, zz, :, cols(s)]

    def quad_of(buf, s, big):
        return buf.at[:, big, :, cols(s)] if s < 2 else buf.at[big, :, :, cols(s)]

    positions = [(x, z), (x, z), (z, x), (z, x)]
    forward = [(1 - 2 * (s % 2)) * (1 - 2 * core) for s in range(4)]

    def shift(pos, by):
        return lax.rem(pos + by + 2 * SIDE, SIDE)

    def on_small(s, by):
        small, big = positions[s]
        return device(shift(x, by), z, core) if s < 2 else device(x, shift(z, by), core)

    def on_big(s, by):
        return device(x, shift(z, by), core) if s < 2 else device(shift(x, by), z, core)

    def send(src, dst, sends, recvs, index, target):
        copy = pltpu.make_async_remote_copy(
            src_ref=src, dst_ref=dst, send_sem=sends.at[index], recv_sem=recvs.at[index],
            device_id=target, device_id_type=MESH,
        )
        copy.start()
        return copy

    gather = {}

    def gather_block(s, n, small, target):
        ref = block_of(s, small, positions[s][1])
        gather[s, n] = send(ref, ref, g_send, g_recv, s * 10 + n, target)

    def gather_quad(s, n, big, target):
        ref = quad_of(grid.at[core], s, big)
        gather[s, n] = send(ref, ref, g_send, g_recv, s * 10 + n, target)

    order = (0, 2, 1, 3)
    for s in order:
        small, big = positions[s]
        gather_block(s, 0, small, on_small(s, forward[s]))
        gather_block(s, 1, small, on_small(s, -forward[s]))
    for s in order:
        small, big = positions[s]
        gather[s, 0].wait_recv()
        gather_block(s, 2, shift(small, -forward[s]), on_small(s, forward[s]))
    for s in order:
        small, big = positions[s]
        gather[s, 1].wait_recv()
        gather[s, 2].wait_recv()
        gather_quad(s, 3, big, on_big(s, forward[s]))
        gather_quad(s, 4, big, on_big(s, -forward[s]))
        gather_quad(s, 6, big, sibling)
    for s in order:
        small, big = positions[s]
        gather[s, 3].wait_recv()
        gather_quad(s, 5, shift(big, -forward[s]), on_big(s, forward[s]))
        gather_quad(s, 7, shift(big, -forward[s]), sibling)

    first = [True]

    def contract(c, turn, s):
        for copy in loads[turn, s]:
            copy.wait()
        rows = pl.ds(pl.multiple_of(c * half + starts[s], LANES), widths[s])
        lhs = grid[c, :, :, :, starts[s] : starts[s] + widths[s]].reshape(ROWS, widths[s])
        for acc, weight in ((gate, wg), (up, wu)):
            product = jnp.dot(lhs, weight[rows, :], preferred_element_type=jnp.float32)
            if first[0]:
                acc[...] = product
            else:
                acc[...] += product
        first[0] = False

    for s in order:
        small, big = positions[s]
        gather[s, 4].wait_recv()
        gather_quad(s, 8, shift(big, forward[s]), sibling)
        gather[s, 5].wait_recv()
        gather_quad(s, 9, shift(big, 2), sibling)
        contract(core, 0, s)
    for s in order:
        for n in (6, 7, 8, 9):
            gather[s, n].wait_recv()
        contract(other, 1, s)

    value = gate[...]
    hidden[...] = (value / (1.0 + jnp.exp(-value)) * up[...]).astype(jnp.bfloat16)
    wd_load.wait()

    scatter = {}

    def partial_cols(c, s):
        col = pl.ds(pl.multiple_of(c * half + starts[s], LANES), widths[s])
        product = jnp.dot(hidden[...], wd[:, col], preferred_element_type=jnp.float32)
        return product.reshape(SIDE, SIDE, CAP, widths[s])

    def load_cols(buf, s):
        return buf[..., starts[s] : starts[s] + widths[s]]

    def start_stream(s):
        c = cols(s)
        pout[:, :, :, c] = partial_cols(other, s).astype(jnp.bfloat16)
        scatter[s, 0] = send(
            pout.at[:, :, :, c], pin.at[:, :, :, c], r_send, r_recv, s * 7, sibling
        )
        mine = partial_cols(core, s)
        scatter[s, 0].wait_recv()
        chip_sum[:, :, :, c] = (mine + pin[:, :, :, c].astype(jnp.float32)).astype(jnp.bfloat16)
        small, big = positions[s]
        d = forward[s]
        scatter[s, 1] = send(
            quad_of(chip_sum, s, shift(big, 2)), big_in.at[0, :, :, c],
            r_send, r_recv, s * 7 + 1, on_big(s, d),
        )
        scatter[s, 2] = send(
            quad_of(chip_sum, s, shift(big, -d)), big_in.at[1, :, :, c],
            r_send, r_recv, s * 7 + 2, on_big(s, -d),
        )

    def quad_load(s, big):
        c = cols(s)
        return (chip_sum[:, big, :, c] if s < 2 else chip_sum[big, :, :, c]).astype(jnp.float32)

    def relay_quad(s):
        c = cols(s)
        small, big = positions[s]
        d = forward[s]
        scatter[s, 1].wait_recv()
        big_in[0, :, :, c] = (
            quad_load(s, shift(big, d)) + big_in[0, :, :, c].astype(jnp.float32)
        ).astype(jnp.bfloat16)
        scatter[s, 3] = send(
            big_in.at[0, :, :, c], big_in.at[2, :, :, c],
            r_send, r_recv, s * 7 + 3, on_big(s, d),
        )

    def start_small(s):
        c = cols(s)
        small, big = positions[s]
        d = forward[s]
        scatter[s, 2].wait_recv()
        scatter[s, 3].wait_recv()
        quad_sum[:, :, c] = (
            quad_load(s, big)
            + big_in[1, :, :, c].astype(jnp.float32)
            + big_in[2, :, :, c].astype(jnp.float32)
        ).astype(jnp.bfloat16)
        scatter[s, 4] = send(
            quad_sum.at[shift(small, 2), :, c], small_in.at[0, :, c],
            r_send, r_recv, s * 7 + 4, on_small(s, d),
        )
        scatter[s, 5] = send(
            quad_sum.at[shift(small, -d), :, c], small_in.at[1, :, c],
            r_send, r_recv, s * 7 + 5, on_small(s, -d),
        )

    def relay_small(s):
        c = cols(s)
        small, big = positions[s]
        d = forward[s]
        scatter[s, 4].wait_recv()
        small_in[0, :, c] = (
            quad_sum[shift(small, d), :, c].astype(jnp.float32)
            + small_in[0, :, c].astype(jnp.float32)
        ).astype(jnp.bfloat16)
        scatter[s, 6] = send(
            small_in.at[0, :, c], small_in.at[2, :, c],
            r_send, r_recv, s * 7 + 6, on_small(s, d),
        )

    def finish_stream(s):
        c = cols(s)
        small, big = positions[s]
        scatter[s, 5].wait_recv()
        scatter[s, 6].wait_recv()
        final[:, c] = (
            quad_sum[small, :, c].astype(jnp.float32)
            + small_in[1, :, c].astype(jnp.float32)
            + small_in[2, :, c].astype(jnp.float32)
        )

    stages = (start_stream, relay_quad, start_small, relay_small, finish_stream)
    for t in range(len(order) + len(stages) - 1):
        for n, stage in enumerate(stages):
            if 0 <= t - n < len(order):
                stage(order[t - n])

    for m in range(hb):
        spread2[pl.ds(m, CAP, stride=rp), :] = final[:, m * LANES : (m + 1) * LANES]
    for k in range(ROWS // CHIPS):
        rows_out[k] = spread2[k * rp : (k + 1) * rp, :].astype(jnp.bfloat16)
    for i in range(DEVICES):
        rank = offs[i] + row_for(chip, offs[i])
        pkt_back[i] = rows_out[jnp.minimum(rank // CHIPS, ROWS // CHIPS - 1)]
    inbox_back[me] = pkt_back[me]

    def send_back(s):
        t = lax.rem(me + s, DEVICES)
        return pltpu.make_async_remote_copy(
            src_ref=pkt_back.at[t], dst_ref=inbox_back.at[me],
            send_sem=b_send.at[s], recv_sem=b_recv.at[me],
            device_id={"tensor": t}, device_id_type=MESH,
        )

    def sent_back(s):
        t = lax.rem(me + s, DEVICES)
        return pltpu.make_async_remote_copy(
            src_ref=pkt_back.at[0], dst_ref=inbox_back.at[t],
            send_sem=b_send.at[s], recv_sem=b_recv.at[t],
            device_id={"tensor": t}, device_id_type=MESH,
        )

    @pl.loop(1, DEVICES)
    def _(s):
        send_back(s).start()

    @pl.loop(1, DEVICES)
    def _(s):
        dispatch(s).wait_send()

    for copy in list(gather.values()) + list(scatter.values()):
        copy.wait_send()

    @pl.loop(1, DEVICES)
    def _(s):
        sent_back(s).wait_recv()

    for j in range(CAP):
        p = lax.rem(my_off + j, CHIPS)
        for h in range(2):
            row = inbox_back[2 * p + h].astype(jnp.float32)
            row = jnp.where(j < my_count, row, jnp.zeros_like(row))
            spread[(2 * j + h) * rp : (2 * j + h + 1) * rp, :] = row
    for h in range(2):
        for m in range(hb):
            block = spread[pl.ds(h * rp + m, CAP, stride=2 * rp), :]
            at = (h * hb + m) * LANES
            out[:, at : at + LANES] = block.astype(jnp.bfloat16)

    @pl.loop(1, DEVICES)
    def _(s):
        send_back(s).wait_send()


def local(requests, counts, gate_weight, up_weight, down_weight):
    capacity, features = requests.shape
    ff = gate_weight.shape[1]
    half = features // 2
    rp = -(-(half // LANES) // 16) * 16
    bf16, f32 = jnp.bfloat16, jnp.float32
    dma = pltpu.SemaphoreType.DMA
    return pl.pallas_call(
        kernel,
        out_shape=jax.ShapeDtypeStruct((capacity, features), bf16),
        in_specs=[
            pl.BlockSpec(memory_space=pltpu.VMEM),
            pl.BlockSpec(memory_space=pltpu.SMEM),
            pl.BlockSpec(memory_space=pl.ANY),
            pl.BlockSpec(memory_space=pl.ANY),
            pl.BlockSpec(memory_space=pl.ANY),
        ],
        out_specs=pl.BlockSpec(memory_space=pltpu.VMEM),
        scratch_shapes=[
            pltpu.VMEM((features, ff), bf16),
            pltpu.VMEM((features, ff), bf16),
            pltpu.VMEM((ff, features), bf16),
            pltpu.VMEM((CAP * 2 * rp, LANES), f32),
            pltpu.VMEM((CAP * rp, LANES), f32),
            pltpu.VMEM((CHIPS, 2, rp, LANES), bf16),
            pltpu.VMEM((CAP, 2, rp, LANES), bf16),
            pltpu.VMEM((DEVICES, rp, LANES), bf16),
            pltpu.VMEM((2, SIDE, SIDE, CAP, half), bf16),
            pltpu.VMEM((ROWS, ff), f32),
            pltpu.VMEM((ROWS, ff), f32),
            pltpu.VMEM((ROWS, ff), bf16),
            pltpu.VMEM((SIDE, SIDE, CAP, half), bf16),
            pltpu.VMEM((SIDE, SIDE, CAP, half), bf16),
            pltpu.VMEM((SIDE, SIDE, CAP, half), bf16),
            pltpu.VMEM((3, SIDE, CAP, half), bf16),
            pltpu.VMEM((SIDE, CAP, half), bf16),
            pltpu.VMEM((3, CAP, half), bf16),
            pltpu.VMEM((CAP, half), f32),
            pltpu.VMEM((ROWS // CHIPS, rp, LANES), bf16),
            pltpu.VMEM((DEVICES, rp, LANES), bf16),
            pltpu.VMEM((DEVICES, rp, LANES), bf16),
            pltpu.SMEM((DEVICES,), jnp.int32),
            dma((17,)),
            dma((DEVICES,)),
            dma((DEVICES,)),
            dma((40,)),
            dma((40,)),
            dma((28,)),
            dma((28,)),
            dma((DEVICES,)),
            dma((DEVICES,)),
        ],
        compiler_params=pltpu.CompilerParams(
            collective_id=0, has_side_effects=True, vmem_limit_bytes=58 * 2**20
        ),
        cost_estimate=pl.CostEstimate(
            flops=6 * ROWS * features * ff, bytes_accessed=6 * features * ff, transcendentals=ROWS * ff
        ),
        name="ffn",
    )(requests, counts, gate_weight, up_weight, down_weight)


def solution(mesh):
    return jax.shard_map(
        local,
        mesh=mesh,
        in_specs=(
            P(("group", "tensor"), None),
            P("group"),
            P(None, "tensor"),
            P(None, "tensor"),
            P("tensor", None),
        ),
        out_specs=P(("group", "tensor"), None),
        check_vma=False,
    )
```

```python
import functools

import jax
import jax.numpy as jnp
from jax import lax
from jax.experimental import pallas as pl
from jax.experimental.pallas import tpu as pltpu
from jax.sharding import PartitionSpec as P

SIDE = 4
CHIPS = SIDE * SIDE
DEVICES = 2 * CHIPS
CAP = 16
ROWS = 256
LANES = 128
MESH = pl.DeviceIdType.MESH


def stream_widths(half):
    tile = 256 if half % 256 == 0 and half >= 1024 else 128
    tiles = half // tile
    first = (tiles + 3) // 4
    pair = tiles // 2
    return [first * tile, (pair - first) * tile] * 2


def kernel(
    req, counts, wgt_hbm, wut_hbm, wd_hbm, out,
    wgu, wd, spread, spread2, pkt, rows_in, inbox, grid, acc, hidden,
    pout, pin, chip_sum, big_in, quad_sum, small_in, final, rows_out, pkt_back, inbox_back, offs,
    w_sem, a_send, a_recv, g_send, g_recv, r_send, r_recv, b_send, b_recv,
):
    features = req.shape[1]
    half = features // 2
    hb = half // LANES
    rp = inbox.shape[1]
    widths = stream_widths(half)
    starts = [sum(widths[:s]) for s in range(4)]
    order = (0, 2, 1, 3)
    ff = wd.shape[0]
    main = ff // LANES * LANES
    tail = ff - main

    me = lax.axis_index("tensor")
    core = lax.rem(me, 2)
    other = 1 - core
    chip = me // 2
    x = chip // SIDE
    z = lax.rem(chip, SIDE)

    def device(xx, zz, cc):
        return {"tensor": (xx * SIDE + zz) * 2 + cc}

    sibling = device(x, z, other)

    barrier = pltpu.get_barrier_semaphore()

    @pl.loop(1, DEVICES)
    def _(s):
        pl.semaphore_signal(
            barrier, inc=1, device_id={"tensor": lax.rem(me + s, DEVICES)}, device_id_type=MESH
        )

    loads = {}
    pieces = (
        (wgt_hbm, 0, main, 0),
        (wut_hbm, 0, main, main),
        (wgt_hbm, main, tail, 2 * main),
        (wut_hbm, main, tail, 2 * main + tail),
    )
    for turn, c in enumerate((core, other)):
        for s in order:
            col = pl.ds(pl.multiple_of(c * half + starts[s], LANES), widths[s])
            loads[turn, s] = []
            for n, (src, at, size, to) in enumerate(pieces):
                copy = pltpu.make_async_copy(
                    src.at[pl.ds(at, size), col], wgu.at[pl.ds(to, size), col],
                    w_sem.at[turn * 16 + s * 4 + n],
                )
                copy.start()
                loads[turn, s].append(copy)
    wd_load = pltpu.make_async_copy(wd_hbm, wd, w_sem.at[32])
    wd_load.start()

    total = jnp.int32(0)
    ends = []
    for i in range(DEVICES):
        offs[i] = total
        total = total + counts[i]
        ends.append(total)
    my_off = offs[me]
    my_count = counts[me]

    spread[...] = jnp.zeros_like(spread)
    for h in range(2):
        for m in range(hb):
            block = req[:, (h * hb + m) * LANES : (h * hb + m + 1) * LANES]
            spread[pl.ds(h * rp + m, CAP, stride=2 * rp), :] = block.astype(jnp.float32)

    def row_for(p, off):
        return lax.rem(p - off + ROWS, CAP)

    for j in range(CAP):
        for h in range(2):
            at = (2 * j + h) * rp
            rows_in[j, h] = spread[at : at + rp, :].astype(jnp.bfloat16)
    for p in range(CHIPS):
        pkt[p] = rows_in[row_for(p, my_off)]
    inbox[me] = pkt[chip, core]

    pl.semaphore_wait(barrier, DEVICES - 1)

    def dispatch(s):
        t = lax.rem(me + s, DEVICES)
        return pltpu.make_async_remote_copy(
            src_ref=pkt.at[t // 2, lax.rem(t, 2)], dst_ref=inbox.at[me],
            send_sem=a_send.at[s], recv_sem=a_recv.at[me],
            device_id={"tensor": t}, device_id_type=MESH,
        )

    def dispatched(s):
        t = lax.rem(me + s, DEVICES)
        return pltpu.make_async_remote_copy(
            src_ref=pkt.at[0, 0], dst_ref=inbox.at[t],
            send_sem=a_send.at[s], recv_sem=a_recv.at[t],
            device_id={"tensor": t}, device_id_type=MESH,
        )

    @pl.loop(1, DEVICES)
    def _(s):
        dispatch(s).start()

    owners = []
    for k in range(ROWS // CHIPS):
        rank = chip + CHIPS * k
        owner = jnp.int32(0)
        for end in ends[:-1]:
            owner = owner + (end <= rank).astype(jnp.int32)
        owners.append(owner)

    @pl.loop(1, DEVICES)
    def _(s):
        dispatched(s).wait_recv()
        dispatch(s).wait_send()

    for k in range(ROWS // CHIPS):
        spread2[k * rp : (k + 1) * rp, :] = inbox[owners[k]].astype(jnp.float32)
    for m in range(hb):
        block = spread2[pl.ds(m, CAP, stride=rp), :].astype(jnp.bfloat16)
        grid[core, x, z, :, m * LANES : (m + 1) * LANES] = block

    def cols(s):
        return pl.ds(starts[s], widths[s])

    def block_of(s, small, big):
        xx, zz = (small, big) if s < 2 else (big, small)
        return grid.at[core, xx, zz, :, cols(s)]

    def quad_of(buf, s, big):
        return buf.at[:, big, :, cols(s)] if s < 2 else buf.at[big, :, :, cols(s)]

    positions = [(x, z), (x, z), (z, x), (z, x)]
    forward = [(1 - 2 * (s % 2)) * (1 - 2 * core) for s in range(4)]

    def shift(pos, by):
        return lax.rem(pos + by + 2 * SIDE, SIDE)

    def on_small(s, by):
        small, big = positions[s]
        return device(shift(x, by), z, core) if s < 2 else device(x, shift(z, by), core)

    def on_big(s, by):
        return device(x, shift(z, by), core) if s < 2 else device(shift(x, by), z, core)

    def send(src, dst, sends, recvs, index, target):
        copy = pltpu.make_async_remote_copy(
            src_ref=src, dst_ref=dst, send_sem=sends.at[index], recv_sem=recvs.at[index],
            device_id=target, device_id_type=MESH,
        )
        copy.start()
        return copy

    gather = {}

    def gather_block(s, n, small, target):
        ref = block_of(s, small, positions[s][1])
        gather[s, n] = send(ref, ref, g_send, g_recv, s * 10 + n, target)

    def gather_quad(s, n, big, target):
        ref = quad_of(grid.at[core], s, big)
        gather[s, n] = send(ref, ref, g_send, g_recv, s * 10 + n, target)

    for s in order:
        small, big = positions[s]
        gather_block(s, 0, small, on_small(s, forward[s]))
        gather_block(s, 1, small, on_small(s, -forward[s]))
    for s in order:
        small, big = positions[s]
        gather[s, 0].wait_recv()
        gather_block(s, 2, shift(small, -forward[s]), on_small(s, forward[s]))
    for s in order:
        small, big = positions[s]
        gather[s, 1].wait_recv()
        gather[s, 2].wait_recv()
        gather_quad(s, 3, big, on_big(s, forward[s]))
        gather_quad(s, 4, big, on_big(s, -forward[s]))
        gather_quad(s, 6, big, sibling)
    for s in order:
        small, big = positions[s]
        gather[s, 3].wait_recv()
        gather_quad(s, 5, shift(big, -forward[s]), on_big(s, forward[s]))
        gather_quad(s, 7, shift(big, -forward[s]), sibling)

    first = [True]

    def contract(c, turn, s):
        for copy in loads[turn, s]:
            copy.wait()
        col = pl.ds(pl.multiple_of(c * half + starts[s], LANES), widths[s])
        lhs = grid[c, :, :, :, starts[s] : starts[s] + widths[s]].reshape(ROWS, widths[s])
        product = lax.dot_general(
            lhs, wgu[:, col], (((1,), (1,)), ((), ())), preferred_element_type=jnp.float32
        )
        if first[0]:
            acc[...] = product
        else:
            acc[...] += product
        first[0] = False

    for s in order:
        small, big = positions[s]
        gather[s, 4].wait_recv()
        gather_quad(s, 8, shift(big, forward[s]), sibling)
        gather[s, 5].wait_recv()
        gather_quad(s, 9, shift(big, 2), sibling)
        contract(core, 0, s)
    for s in order:
        for n in (6, 7, 8, 9):
            gather[s, n].wait_recv()
        contract(other, 1, s)

    def activate(gate, up):
        return (gate / (1.0 + jnp.exp(-gate)) * up).astype(jnp.bfloat16)

    if main:
        hidden[:, :main] = activate(acc[:, :main], acc[:, main : 2 * main])
    if tail:
        ends_of = acc[:, 2 * main :]
        hidden[:, main:] = activate(ends_of[:, :tail], ends_of[:, tail:])
    wd_load.wait()

    scatter = {}

    def partial_cols(c, s):
        col = pl.ds(pl.multiple_of(c * half + starts[s], LANES), widths[s])
        product = jnp.dot(hidden[...], wd[:, col], preferred_element_type=jnp.float32)
        return product.reshape(SIDE, SIDE, CAP, widths[s])

    def load_cols(buf, s):
        return buf[..., starts[s] : starts[s] + widths[s]]

    def start_stream(s):
        c = cols(s)
        pout[:, :, :, c] = partial_cols(other, s).astype(jnp.bfloat16)
        scatter[s, 0] = send(
            pout.at[:, :, :, c], pin.at[:, :, :, c], r_send, r_recv, s * 7, sibling
        )
        mine = partial_cols(core, s)
        scatter[s, 0].wait_recv()
        chip_sum[:, :, :, c] = (mine + pin[:, :, :, c].astype(jnp.float32)).astype(jnp.bfloat16)
        small, big = positions[s]
        d = forward[s]
        scatter[s, 1] = send(
            quad_of(chip_sum, s, shift(big, 2)), big_in.at[0, :, :, c],
            r_send, r_recv, s * 7 + 1, on_big(s, d),
        )
        scatter[s, 2] = send(
            quad_of(chip_sum, s, shift(big, -d)), big_in.at[1, :, :, c],
            r_send, r_recv, s * 7 + 2, on_big(s, -d),
        )

    def quad_load(s, big):
        c = cols(s)
        return (chip_sum[:, big, :, c] if s < 2 else chip_sum[big, :, :, c]).astype(jnp.float32)

    def relay_quad(s):
        c = cols(s)
        small, big = positions[s]
        d = forward[s]
        scatter[s, 1].wait_recv()
        big_in[0, :, :, c] = (
            quad_load(s, shift(big, d)) + big_in[0, :, :, c].astype(jnp.float32)
        ).astype(jnp.bfloat16)
        scatter[s, 3] = send(
            big_in.at[0, :, :, c], big_in.at[2, :, :, c],
            r_send, r_recv, s * 7 + 3, on_big(s, d),
        )

    def start_small(s):
        c = cols(s)
        small, big = positions[s]
        d = forward[s]
        scatter[s, 2].wait_recv()
        scatter[s, 3].wait_recv()
        quad_sum[:, :, c] = (
            quad_load(s, big)
            + big_in[1, :, :, c].astype(jnp.float32)
            + big_in[2, :, :, c].astype(jnp.float32)
        ).astype(jnp.bfloat16)
        scatter[s, 4] = send(
            quad_sum.at[shift(small, 2), :, c], small_in.at[0, :, c],
            r_send, r_recv, s * 7 + 4, on_small(s, d),
        )
        scatter[s, 5] = send(
            quad_sum.at[shift(small, -d), :, c], small_in.at[1, :, c],
            r_send, r_recv, s * 7 + 5, on_small(s, -d),
        )

    def relay_small(s):
        c = cols(s)
        small, big = positions[s]
        d = forward[s]
        scatter[s, 4].wait_recv()
        small_in[0, :, c] = (
            quad_sum[shift(small, d), :, c].astype(jnp.float32)
            + small_in[0, :, c].astype(jnp.float32)
        ).astype(jnp.bfloat16)
        scatter[s, 6] = send(
            small_in.at[0, :, c], small_in.at[2, :, c],
            r_send, r_recv, s * 7 + 6, on_small(s, d),
        )

    def finish_stream(s):
        c = cols(s)
        small, big = positions[s]
        scatter[s, 5].wait_recv()
        scatter[s, 6].wait_recv()
        final[:, c] = (
            quad_sum[small, :, c].astype(jnp.float32)
            + small_in[1, :, c].astype(jnp.float32)
            + small_in[2, :, c].astype(jnp.float32)
        )

    stages = (start_stream, relay_quad, start_small, relay_small, finish_stream)
    for t in range(len(order) + len(stages) - 1):
        for n, stage in enumerate(stages):
            if 0 <= t - n < len(order):
                stage(order[t - n])

    for m in range(hb):
        spread2[pl.ds(m, CAP, stride=rp), :] = final[:, m * LANES : (m + 1) * LANES]
    for k in range(ROWS // CHIPS):
        rows_out[k] = spread2[k * rp : (k + 1) * rp, :].astype(jnp.bfloat16)
    for i in range(DEVICES):
        rank = offs[i] + row_for(chip, offs[i])
        pkt_back[i] = rows_out[jnp.minimum(rank // CHIPS, ROWS // CHIPS - 1)]
    inbox_back[me] = pkt_back[me]

    def send_back(s):
        t = lax.rem(me + s, DEVICES)
        return pltpu.make_async_remote_copy(
            src_ref=pkt_back.at[t], dst_ref=inbox_back.at[me],
            send_sem=b_send.at[s], recv_sem=b_recv.at[me],
            device_id={"tensor": t}, device_id_type=MESH,
        )

    def sent_back(s):
        t = lax.rem(me + s, DEVICES)
        return pltpu.make_async_remote_copy(
            src_ref=pkt_back.at[0], dst_ref=inbox_back.at[t],
            send_sem=b_send.at[s], recv_sem=b_recv.at[t],
            device_id={"tensor": t}, device_id_type=MESH,
        )

    @pl.loop(1, DEVICES)
    def _(s):
        send_back(s).start()

    for copy in list(gather.values()) + list(scatter.values()):
        copy.wait_send()

    @pl.loop(1, DEVICES)
    def _(s):
        sent_back(s).wait_recv()

    for j in range(CAP):
        p = lax.rem(my_off + j, CHIPS)
        for h in range(2):
            row = inbox_back[2 * p + h].astype(jnp.float32)
            row = jnp.where(j < my_count, row, jnp.zeros_like(row))
            spread[(2 * j + h) * rp : (2 * j + h + 1) * rp, :] = row
    for h in range(2):
        for m in range(hb):
            block = spread[pl.ds(h * rp + m, CAP, stride=2 * rp), :]
            at = (h * hb + m) * LANES
            out[:, at : at + LANES] = block.astype(jnp.bfloat16)

    @pl.loop(1, DEVICES)
    def _(s):
        send_back(s).wait_send()


def local(requests, counts, gate_weight, up_weight, down_weight):
    capacity, features = requests.shape
    ff = gate_weight.shape[1]
    half = features // 2
    rp = -(-(half // LANES) // 16) * 16
    bf16, f32 = jnp.bfloat16, jnp.float32
    dma = pltpu.SemaphoreType.DMA
    return pl.pallas_call(
        kernel,
        out_shape=jax.ShapeDtypeStruct((capacity, features), bf16),
        in_specs=[
            pl.BlockSpec(memory_space=pltpu.VMEM),
            pl.BlockSpec(memory_space=pltpu.SMEM),
            pl.BlockSpec(memory_space=pl.ANY),
            pl.BlockSpec(memory_space=pl.ANY),
            pl.BlockSpec(memory_space=pl.ANY),
        ],
        out_specs=pl.BlockSpec(memory_space=pltpu.VMEM),
        scratch_shapes=[
            pltpu.VMEM((2 * ff, features), bf16),
            pltpu.VMEM((ff, features), bf16),
            pltpu.VMEM((CAP * 2 * rp, LANES), f32),
            pltpu.VMEM((CAP * rp, LANES), f32),
            pltpu.VMEM((CHIPS, 2, rp, LANES), bf16),
            pltpu.VMEM((CAP, 2, rp, LANES), bf16),
            pltpu.VMEM((DEVICES, rp, LANES), bf16),
            pltpu.VMEM((2, SIDE, SIDE, CAP, half), bf16),
            pltpu.VMEM((ROWS, 2 * ff), f32),
            pltpu.VMEM((ROWS, ff), bf16),
            pltpu.VMEM((SIDE, SIDE, CAP, half), bf16),
            pltpu.VMEM((SIDE, SIDE, CAP, half), bf16),
            pltpu.VMEM((SIDE, SIDE, CAP, half), bf16),
            pltpu.VMEM((3, SIDE, CAP, half), bf16),
            pltpu.VMEM((SIDE, CAP, half), bf16),
            pltpu.VMEM((3, CAP, half), bf16),
            pltpu.VMEM((CAP, half), f32),
            pltpu.VMEM((ROWS // CHIPS, rp, LANES), bf16),
            pltpu.VMEM((DEVICES, rp, LANES), bf16),
            pltpu.VMEM((DEVICES, rp, LANES), bf16),
            pltpu.SMEM((DEVICES,), jnp.int32),
            dma((33,)),
            dma((DEVICES,)),
            dma((DEVICES,)),
            dma((40,)),
            dma((40,)),
            dma((28,)),
            dma((28,)),
            dma((DEVICES,)),
            dma((DEVICES,)),
        ],
        compiler_params=pltpu.CompilerParams(
            collective_id=0, has_side_effects=True, vmem_limit_bytes=58 * 2**20
        ),
        cost_estimate=pl.CostEstimate(
            flops=6 * ROWS * features * ff, bytes_accessed=6 * features * ff, transcendentals=ROWS * ff
        ),
        name="ffn",
    )(requests, counts, gate_weight.T, up_weight.T, down_weight)


def solution(mesh):
    return jax.shard_map(
        local,
        mesh=mesh,
        in_specs=(
            P(("group", "tensor"), None),
            P("group"),
            P(None, "tensor"),
            P(None, "tensor"),
            P("tensor", None),
        ),
        out_specs=P(("group", "tensor"), None),
        check_vma=False,
    )
```

```python
import functools

import jax
import jax.numpy as jnp
from jax import lax
from jax.experimental import pallas as pl
from jax.experimental.pallas import tpu as pltpu
from jax.sharding import PartitionSpec as P

SIDE = 4
CHIPS = SIDE * SIDE
DEVICES = 2 * CHIPS
CAP = 16
ROWS = 256
LANES = 128
MESH = pl.DeviceIdType.MESH


def column_pieces(half):
    tile = 256 if half % 512 == 0 and half >= 1024 else 128
    per_order = half // tile // 2
    pieces = []
    for n in range((per_order + 1) // 2):
        for turned in range(2):
            at = (turned * per_order + 2 * n) * tile
            pieces.append((at, min(2, per_order - 2 * n) * tile, turned, n % 2))
    return pieces


def kernel(
    req, counts, wgt_hbm, wut_hbm, wd_hbm, out,
    wgu, wd, spread, spread2, pkt, rows_in, inbox, grid, acc, hidden,
    pout, pin, chip_sum, big_in, quad_sum, small_in, final, rows_out, pkt_back, inbox_back, offs,
    w_sem, a_send, a_recv, g_send, g_recv, r_send, r_recv, b_send, b_recv,
):
    features = req.shape[1]
    half = features // 2
    hb = half // LANES
    rp = inbox.shape[1]
    pieces = column_pieces(half)
    order = range(len(pieces))
    ff = wd.shape[0]
    main = ff // LANES * LANES
    tail = ff - main

    me = lax.axis_index("tensor")
    core = lax.rem(me, 2)
    other = 1 - core
    chip = me // 2
    x = chip // SIDE
    z = lax.rem(chip, SIDE)

    def device(xx, zz, cc):
        return {"tensor": (xx * SIDE + zz) * 2 + cc}

    sibling = device(x, z, other)

    hops = (0, 1, 2, 1)
    others = sorted(
        ((dx, dz, dc) for dx in range(SIDE) for dz in range(SIDE) for dc in range(2) if dx or dz or dc),
        key=lambda o: -hops[o[0]] - hops[o[1]],
    )

    def at_offset(o, sign):
        xx = lax.rem(x + sign * o[0] + SIDE, SIDE)
        zz = lax.rem(z + sign * o[1] + SIDE, SIDE)
        return xx * SIDE + zz, lax.rem(core + o[2], 2)

    def exchange(source, box, sends, recvs):
        copies = []
        for n, o in enumerate(others):
            to_chip, to_core = at_offset(o, 1)
            copy = pltpu.make_async_remote_copy(
                src_ref=source(to_chip, to_core), dst_ref=box.at[me],
                send_sem=sends.at[n], recv_sem=recvs.at[me],
                device_id={"tensor": 2 * to_chip + to_core}, device_id_type=MESH,
            )
            copy.start()
            copies.append(copy)
        return copies

    def arrived(box, sends, recvs):
        for n, o in enumerate(others):
            from_chip, from_core = at_offset(o, -1)
            origin = 2 * from_chip + from_core
            pltpu.make_async_remote_copy(
                src_ref=box.at[me], dst_ref=box.at[origin],
                send_sem=sends.at[n], recv_sem=recvs.at[origin],
                device_id={"tensor": origin}, device_id_type=MESH,
            ).wait_recv()

    barrier = pltpu.get_barrier_semaphore()

    @pl.loop(1, DEVICES)
    def _(s):
        pl.semaphore_signal(
            barrier, inc=1, device_id={"tensor": lax.rem(me + s, DEVICES)}, device_id_type=MESH
        )

    loads = []
    for n, (src, at, size, to) in enumerate((
        (wgt_hbm, 0, main, 0),
        (wut_hbm, 0, main, main),
        (wgt_hbm, main, tail, 2 * main),
        (wut_hbm, main, tail, 2 * main + tail),
    )):
        if size:
            loads.append(
                pltpu.make_async_copy(src.at[pl.ds(at, size)], wgu.at[pl.ds(to, size)], w_sem.at[n])
            )
            loads[-1].start()
    wd_load = pltpu.make_async_copy(wd_hbm, wd, w_sem.at[4])
    wd_load.start()

    total = jnp.int32(0)
    ends = []
    for i in range(DEVICES):
        offs[i] = total
        total = total + counts[i]
        ends.append(total)
    my_off = offs[me]
    my_count = counts[me]

    spread[...] = jnp.zeros_like(spread)
    for h in range(2):
        for m in range(hb):
            block = req[:, (h * hb + m) * LANES : (h * hb + m + 1) * LANES]
            spread[pl.ds(h * rp + m, CAP, stride=2 * rp), :] = block.astype(jnp.float32)

    def row_for(p, off):
        return lax.rem(p - off + ROWS, CAP)

    for j in range(CAP):
        for h in range(2):
            at = (2 * j + h) * rp
            rows_in[j, h] = spread[at : at + rp, :].astype(jnp.bfloat16)
    for p in range(CHIPS):
        pkt[p] = rows_in[row_for(p, my_off)]
    inbox[me] = pkt[chip, core]

    pl.semaphore_wait(barrier, DEVICES - 1)

    dispatched = exchange(lambda p, c: pkt.at[p, c], inbox, a_send, a_recv)

    owners = []
    for k in range(ROWS // CHIPS):
        rank = chip + CHIPS * k
        owner = jnp.int32(0)
        for end in ends[:-1]:
            owner = owner + (end <= rank).astype(jnp.int32)
        owners.append(owner)

    arrived(inbox, a_send, a_recv)

    for k in range(ROWS // CHIPS):
        spread2[k * rp : (k + 1) * rp, :] = inbox[owners[k]].astype(jnp.float32)
    for m in range(hb):
        block = spread2[pl.ds(m, CAP, stride=rp), :].astype(jnp.bfloat16)
        grid[core, x, z, :, m * LANES : (m + 1) * LANES] = block

    def cols(s):
        return pl.ds(pieces[s][0], pieces[s][1])

    def turned(s):
        return pieces[s][2]

    def quad_of(buf, s, big):
        return buf.at[big, :, :, cols(s)] if turned(s) else buf.at[:, big, :, cols(s)]

    positions = [(z, x) if turned(s) else (x, z) for s in order]
    forward = [(1 - 2 * pieces[s][3]) * (1 - 2 * core) for s in order]

    def shift(pos, by):
        return lax.rem(pos + by + 2 * SIDE, SIDE)

    def on_small(s, by):
        return device(x, shift(z, by), core) if turned(s) else device(shift(x, by), z, core)

    def on_big(s, by):
        return device(shift(x, by), z, core) if turned(s) else device(x, shift(z, by), core)

    def send(src, dst, sends, recvs, index, target):
        copy = pltpu.make_async_remote_copy(
            src_ref=src, dst_ref=dst, send_sem=sends.at[index], recv_sem=recvs.at[index],
            device_id=target, device_id_type=MESH,
        )
        copy.start()
        return copy

    gather = {}

    def gather_quad(s, n, big, target):
        ref = quad_of(grid.at[core], s, big)
        gather[s, n] = send(ref, ref, g_send, g_recv, s * 10 + n, target)

    for s in order:
        ref = grid.at[core, x, z, :, cols(s)]
        for by in range(1, SIDE):
            gather[s, by - 1] = send(ref, ref, g_send, g_recv, s * 10 + by - 1, on_small(s, by))
    for s in order:
        big = positions[s][1]
        for n in range(3):
            gather[s, n].wait_recv()
        gather_quad(s, 3, big, on_big(s, forward[s]))
        gather_quad(s, 4, big, on_big(s, -forward[s]))
        gather_quad(s, 6, big, sibling)
    for s in order:
        behind = shift(positions[s][1], -forward[s])
        gather[s, 3].wait_recv()
        gather_quad(s, 5, behind, on_big(s, forward[s]))
        gather_quad(s, 7, behind, sibling)

    for copy in loads:
        copy.wait()

    def contract(c, s):
        at, width = pieces[s][:2]
        col = pl.ds(pl.multiple_of(c * half + at, LANES), width)
        lhs = grid[c, :, :, :, at : at + width].reshape(ROWS, width)
        return lax.dot_general(
            lhs, wgu[:, col], (((1,), (1,)), ((), ())), preferred_element_type=jnp.float32
        )

    def contract_sibling(s):
        for n in (6, 7, 8, 9):
            gather[s, n].wait_recv()
        acc[...] += contract(other, s)

    for s in order:
        big = positions[s][1]
        gather[s, 4].wait_recv()
        gather_quad(s, 8, shift(big, forward[s]), sibling)
        gather[s, 5].wait_recv()
        gather_quad(s, 9, shift(big, 2), sibling)
        if s == 0:
            acc[...] = contract(core, s)
        else:
            acc[...] += contract(core, s)
            contract_sibling(s - 1)
    contract_sibling(len(pieces) - 1)

    def activate(gate, up):
        return (gate / (1.0 + jnp.exp(-gate)) * up).astype(jnp.bfloat16)

    if main:
        hidden[:, :main] = activate(acc[:, :main], acc[:, main : 2 * main])
    if tail:
        ends_of = acc[:, 2 * main :]
        hidden[:, main:] = activate(ends_of[:, :tail], ends_of[:, tail:])
    wd_load.wait()

    scatter = {}

    def partial_cols(c, s):
        at, width = pieces[s][:2]
        col = pl.ds(pl.multiple_of(c * half + at, LANES), width)
        product = jnp.dot(hidden[...], wd[:, col], preferred_element_type=jnp.float32)
        return product.reshape(SIDE, SIDE, CAP, width)

    def scatter_send(s, n, src, dst, target):
        scatter[s, n] = send(src, dst, r_send, r_recv, s * 7 + n, target)

    def to_sibling(s):
        c = cols(s)
        pout[:, :, :, c] = partial_cols(other, s).astype(jnp.bfloat16)
        scatter_send(s, 0, pout.at[:, :, :, c], pin.at[:, :, :, c], sibling)

    def add_cores(s):
        c = cols(s)
        big, d = positions[s][1], forward[s]
        mine = partial_cols(core, s)
        scatter[s, 0].wait_recv()
        chip_sum[:, :, :, c] = (mine + pin[:, :, :, c].astype(jnp.float32)).astype(jnp.bfloat16)
        scatter_send(s, 1, quad_of(chip_sum, s, shift(big, 2)), big_in.at[0, :, :, c], on_big(s, d))
        scatter_send(s, 2, quad_of(chip_sum, s, shift(big, -d)), big_in.at[1, :, :, c], on_big(s, -d))

    def quad_load(s, big):
        c = cols(s)
        return (chip_sum[big, :, :, c] if turned(s) else chip_sum[:, big, :, c]).astype(jnp.float32)

    def relay_quad(s):
        c = cols(s)
        big, d = positions[s][1], forward[s]
        scatter[s, 1].wait_recv()
        big_in[0, :, :, c] = (
            quad_load(s, shift(big, d)) + big_in[0, :, :, c].astype(jnp.float32)
        ).astype(jnp.bfloat16)
        scatter_send(s, 3, big_in.at[0, :, :, c], big_in.at[2, :, :, c], on_big(s, d))

    def start_small(s):
        c = cols(s)
        small, big = positions[s]
        scatter[s, 2].wait_recv()
        scatter[s, 3].wait_recv()
        quad_sum[:, :, c] = (
            quad_load(s, big)
            + big_in[1, :, :, c].astype(jnp.float32)
            + big_in[2, :, :, c].astype(jnp.float32)
        ).astype(jnp.bfloat16)
        for by in range(1, SIDE):
            scatter_send(
                s, 3 + by, quad_sum.at[shift(small, by), :, c], small_in.at[by - 1, :, c], on_small(s, by)
            )

    def finish(s):
        c = cols(s)
        small = positions[s][0]
        value = quad_sum[small, :, c].astype(jnp.float32)
        for n in range(SIDE - 1):
            scatter[s, 4 + n].wait_recv()
            value = value + small_in[n, :, c].astype(jnp.float32)
        final[:, c] = value

    to_sibling(0)
    for s in order:
        if s + 1 < len(pieces):
            to_sibling(s + 1)
        add_cores(s)
    for stage in (relay_quad, start_small, finish):
        for s in order:
            stage(s)

    for m in range(hb):
        spread2[pl.ds(m, CAP, stride=rp), :] = final[:, m * LANES : (m + 1) * LANES]
    for k in range(ROWS // CHIPS):
        rows_out[k] = spread2[k * rp : (k + 1) * rp, :].astype(jnp.bfloat16)
    for i in range(DEVICES):
        rank = offs[i] + row_for(chip, offs[i])
        pkt_back[i] = rows_out[jnp.minimum(rank // CHIPS, ROWS // CHIPS - 1)]
    inbox_back[me] = pkt_back[me]

    returned = exchange(lambda p, c: pkt_back.at[2 * p + c], inbox_back, b_send, b_recv)

    for copy in dispatched + list(gather.values()) + list(scatter.values()):
        copy.wait_send()
    arrived(inbox_back, b_send, b_recv)

    for j in range(CAP):
        p = lax.rem(my_off + j, CHIPS)
        for h in range(2):
            row = inbox_back[2 * p + h].astype(jnp.float32)
            row = jnp.where(j < my_count, row, jnp.zeros_like(row))
            spread[(2 * j + h) * rp : (2 * j + h + 1) * rp, :] = row
    for h in range(2):
        for m in range(hb):
            block = spread[pl.ds(h * rp + m, CAP, stride=2 * rp), :]
            at = (h * hb + m) * LANES
            out[:, at : at + LANES] = block.astype(jnp.bfloat16)
    for copy in returned:
        copy.wait_send()


def local(requests, counts, gate_weight, up_weight, down_weight):
    capacity, features = requests.shape
    ff = gate_weight.shape[1]
    half = features // 2
    n_pieces = len(column_pieces(half))
    rp = -(-(half // LANES) // 16) * 16
    bf16, f32 = jnp.bfloat16, jnp.float32
    dma = pltpu.SemaphoreType.DMA
    return pl.pallas_call(
        kernel,
        out_shape=jax.ShapeDtypeStruct((capacity, features), bf16),
        in_specs=[
            pl.BlockSpec(memory_space=pltpu.VMEM),
            pl.BlockSpec(memory_space=pltpu.SMEM),
            pl.BlockSpec(memory_space=pl.ANY),
            pl.BlockSpec(memory_space=pl.ANY),
            pl.BlockSpec(memory_space=pl.ANY),
        ],
        out_specs=pl.BlockSpec(memory_space=pltpu.VMEM),
        scratch_shapes=[
            pltpu.VMEM((2 * ff, features), bf16),
            pltpu.VMEM((ff, features), bf16),
            pltpu.VMEM((CAP * 2 * rp, LANES), f32),
            pltpu.VMEM((CAP * rp, LANES), f32),
            pltpu.VMEM((CHIPS, 2, rp, LANES), bf16),
            pltpu.VMEM((CAP, 2, rp, LANES), bf16),
            pltpu.VMEM((DEVICES, rp, LANES), bf16),
            pltpu.VMEM((2, SIDE, SIDE, CAP, half), bf16),
            pltpu.VMEM((ROWS, 2 * ff), f32),
            pltpu.VMEM((ROWS, ff), bf16),
            pltpu.VMEM((SIDE, SIDE, CAP, half), bf16),
            pltpu.VMEM((SIDE, SIDE, CAP, half), bf16),
            pltpu.VMEM((SIDE, SIDE, CAP, half), bf16),
            pltpu.VMEM((3, SIDE, CAP, half), bf16),
            pltpu.VMEM((SIDE, CAP, half), bf16),
            pltpu.VMEM((3, CAP, half), bf16),
            pltpu.VMEM((CAP, half), f32),
            pltpu.VMEM((ROWS // CHIPS, rp, LANES), bf16),
            pltpu.VMEM((DEVICES, rp, LANES), bf16),
            pltpu.VMEM((DEVICES, rp, LANES), bf16),
            pltpu.SMEM((DEVICES,), jnp.int32),
            dma((5,)),
            dma((DEVICES,)),
            dma((DEVICES,)),
            dma((n_pieces * 10,)),
            dma((n_pieces * 10,)),
            dma((n_pieces * 7,)),
            dma((n_pieces * 7,)),
            dma((DEVICES,)),
            dma((DEVICES,)),
        ],
        compiler_params=pltpu.CompilerParams(
            collective_id=0, has_side_effects=True, vmem_limit_bytes=58 * 2**20
        ),
        cost_estimate=pl.CostEstimate(
            flops=6 * ROWS * features * ff, bytes_accessed=6 * features * ff, transcendentals=ROWS * ff
        ),
        name="ffn",
    )(requests, counts, gate_weight.T, up_weight.T, down_weight)


def solution(mesh):
    return jax.shard_map(
        local,
        mesh=mesh,
        in_specs=(
            P(("group", "tensor"), None),
            P("group"),
            P(None, "tensor"),
            P(None, "tensor"),
            P("tensor", None),
        ),
        out_specs=P(("group", "tensor"), None),
        check_vma=False,
    )
```

```python
import functools

import jax
import jax.numpy as jnp
from jax import lax
from jax.experimental import pallas as pl
from jax.experimental.pallas import tpu as pltpu
from jax.sharding import PartitionSpec as P

SIDE = 4
CHIPS = SIDE * SIDE
DEVICES = 2 * CHIPS
CAP = 16
ROWS = 256
LANES = 128
MESH = pl.DeviceIdType.MESH


def column_pieces(half):
    tile = 256 if half % 512 == 0 and half >= 1024 else 128
    per_order = half // tile // 2
    pieces = []
    for n in range((per_order + 1) // 2):
        for turned in range(2):
            at = (turned * per_order + 2 * n) * tile
            pieces.append((at, min(2, per_order - 2 * n) * tile, turned, n % 2))
    return pieces


def kernel(
    req_hbm, counts, wgt_hbm, wut_hbm, wd_hbm, out,
    req, wgu, wd, spread, spread2, pkt, rows_in, inbox, grid, acc, hidden,
    chip_sum, big_in, quad_sum, small_in, final, rows_out, pkt_back, inbox_back, offs,
    w_sem, s_send, s_recv, a_send, a_recv, g_send, g_recv, r_send, r_recv, b_send, b_recv,
):
    features = req.shape[1]
    half = features // 2
    hb = half // LANES
    rp = inbox.shape[1]
    pieces = column_pieces(half)
    order = range(len(pieces))
    ff = wd.shape[1]
    main = ff // LANES * LANES
    tail = ff - main

    me = lax.axis_index("tensor")
    core = lax.rem(me, 2)
    other = 1 - core
    chip = me // 2
    x = chip // SIDE
    z = lax.rem(chip, SIDE)

    def device(xx, zz, cc):
        return {"tensor": (xx * SIDE + zz) * 2 + cc}

    sibling = device(x, z, other)

    hops = (0, 1, 2, 1)
    others = sorted(
        ((dx, dz, dc) for dx in range(SIDE) for dz in range(SIDE) for dc in range(2) if dx or dz or dc),
        key=lambda o: -hops[o[0]] - hops[o[1]],
    )

    def at_offset(o, sign):
        xx = lax.rem(x + sign * o[0] + SIDE, SIDE)
        zz = lax.rem(z + sign * o[1] + SIDE, SIDE)
        return xx * SIDE + zz, lax.rem(core + o[2], 2)

    def exchange(source, box, sends, recvs):
        copies = []
        for n, o in enumerate(others):
            to_chip, to_core = at_offset(o, 1)
            copy = pltpu.make_async_remote_copy(
                src_ref=source(to_chip, to_core), dst_ref=box.at[me],
                send_sem=sends.at[n], recv_sem=recvs.at[me],
                device_id={"tensor": 2 * to_chip + to_core}, device_id_type=MESH,
            )
            copy.start()
            copies.append(copy)
        return copies

    def arrived(box, sends, recvs):
        for n, o in enumerate(others):
            from_chip, from_core = at_offset(o, -1)
            origin = 2 * from_chip + from_core
            pltpu.make_async_remote_copy(
                src_ref=box.at[me], dst_ref=box.at[origin],
                send_sem=sends.at[n], recv_sem=recvs.at[origin],
                device_id={"tensor": origin}, device_id_type=MESH,
            ).wait_recv()

    req_load = pltpu.make_async_copy(req_hbm, req, w_sem.at[5])
    req_load.start()

    barrier = pltpu.get_barrier_semaphore()

    @pl.loop(1, DEVICES)
    def _(s):
        pl.semaphore_signal(
            barrier, inc=1, device_id={"tensor": lax.rem(me + s, DEVICES)}, device_id_type=MESH
        )

    loads = []
    for n, (src, at, size, to) in enumerate((
        (wgt_hbm, 0, main, 0),
        (wut_hbm, 0, main, main),
        (wgt_hbm, main, tail, 2 * main),
        (wut_hbm, main, tail, 2 * main + tail),
    )):
        if size:
            loads.append(
                pltpu.make_async_copy(src.at[pl.ds(at, size)], wgu.at[pl.ds(to, size)], w_sem.at[n])
            )
            loads[-1].start()
    wd_load = pltpu.make_async_copy(
        wd_hbm.at[:, pl.ds(pl.multiple_of(core * half, LANES), half)], wd.at[0], w_sem.at[4]
    )
    wd_load.start()

    total = jnp.int32(0)
    ends = []
    for i in range(DEVICES):
        offs[i] = total
        total = total + counts[i]
        ends.append(total)
    my_off = offs[me]
    my_count = counts[me]

    spread[...] = jnp.zeros_like(spread)
    req_load.wait()
    for h in range(2):
        for m in range(hb):
            block = req[:, (h * hb + m) * LANES : (h * hb + m + 1) * LANES]
            spread[pl.ds(h * rp + m, CAP, stride=2 * rp), :] = block.astype(jnp.float32)

    def row_for(p, off):
        return lax.rem(p - off + ROWS, CAP)

    for j in range(CAP):
        for h in range(2):
            at = (2 * j + h) * rp
            rows_in[j, h] = spread[at : at + rp, :].astype(jnp.bfloat16)
    for p in range(CHIPS):
        pkt[p] = rows_in[row_for(p, my_off)]
    inbox[me] = pkt[chip, core]

    pl.semaphore_wait(barrier, DEVICES - 1)

    wd_share = pltpu.make_async_remote_copy(
        src_ref=wd_hbm.at[:, pl.ds(pl.multiple_of(other * half, LANES), half)], dst_ref=wd.at[1],
        send_sem=s_send.at[0], recv_sem=s_recv.at[0], device_id=sibling, device_id_type=MESH,
    )
    dispatched = exchange(lambda p, c: pkt.at[p, c], inbox, a_send, a_recv)

    wd_share.start()

    owners = []
    for k in range(ROWS // CHIPS):
        rank = chip + CHIPS * k
        owner = jnp.int32(0)
        for end in ends[:-1]:
            owner = owner + (end <= rank).astype(jnp.int32)
        owners.append(owner)

    arrived(inbox, a_send, a_recv)

    for k in range(ROWS // CHIPS):
        spread2[k * rp : (k + 1) * rp, :] = inbox[owners[k]].astype(jnp.float32)
    for m in range(hb):
        block = spread2[pl.ds(m, CAP, stride=rp), :].astype(jnp.bfloat16)
        grid[core, x, z, :, m * LANES : (m + 1) * LANES] = block

    def cols(s):
        return pl.ds(pieces[s][0], pieces[s][1])

    def turned(s):
        return pieces[s][2]

    def quad_of(buf, s, big):
        return buf.at[big, :, :, cols(s)] if turned(s) else buf.at[:, big, :, cols(s)]

    positions = [(z, x) if turned(s) else (x, z) for s in order]
    forward = [(1 - 2 * pieces[s][3]) * (1 - 2 * core) for s in order]

    def shift(pos, by):
        return lax.rem(pos + by + 2 * SIDE, SIDE)

    def on_small(s, by):
        return device(x, shift(z, by), core) if turned(s) else device(shift(x, by), z, core)

    def on_big(s, by):
        return device(shift(x, by), z, core) if turned(s) else device(x, shift(z, by), core)

    def send(src, dst, sends, recvs, index, target):
        copy = pltpu.make_async_remote_copy(
            src_ref=src, dst_ref=dst, send_sem=sends.at[index], recv_sem=recvs.at[index],
            device_id=target, device_id_type=MESH,
        )
        copy.start()
        return copy

    gather = {}

    def gather_quad(s, n, big, target):
        ref = quad_of(grid.at[core], s, big)
        gather[s, n] = send(ref, ref, g_send, g_recv, s * 10 + n, target)

    for s in order:
        ref = grid.at[core, x, z, :, cols(s)]
        for by in range(1, SIDE):
            gather[s, by - 1] = send(ref, ref, g_send, g_recv, s * 10 + by - 1, on_small(s, by))
    for s in order:
        big = positions[s][1]
        for n in range(3):
            gather[s, n].wait_recv()
        gather_quad(s, 3, big, on_big(s, forward[s]))
        gather_quad(s, 4, big, on_big(s, -forward[s]))
        gather_quad(s, 6, big, sibling)
    for s in order:
        behind = shift(positions[s][1], -forward[s])
        gather[s, 3].wait_recv()
        gather_quad(s, 5, behind, on_big(s, forward[s]))
        gather_quad(s, 7, behind, sibling)

    for copy in loads:
        copy.wait()

    def contract(c, s):
        at, width = pieces[s][:2]
        col = pl.ds(pl.multiple_of(c * half + at, LANES), width)
        lhs = grid[c, :, :, :, at : at + width].reshape(ROWS, width)
        return lax.dot_general(
            lhs, wgu[:, col], (((1,), (1,)), ((), ())), preferred_element_type=jnp.float32
        )

    def arrive(s):
        big = positions[s][1]
        gather[s, 4].wait_recv()
        gather_quad(s, 8, shift(big, forward[s]), sibling)
        gather[s, 5].wait_recv()
        gather_quad(s, 9, shift(big, 2), sibling)

    def from_sibling(s):
        for n in (6, 7, 8, 9):
            gather[s, n].wait_recv()

    first, second = order[: len(pieces) // 2], order[len(pieces) // 2 :]
    for s in first:
        arrive(s)
    acc[...] = sum(contract(core, s) for s in first)
    for s in second:
        arrive(s)
    for s in first:
        from_sibling(s)
    acc[...] += sum([contract(core, s) for s in second] + [contract(other, s) for s in first])
    for s in second:
        from_sibling(s)
    acc[...] += sum(contract(other, s) for s in second)

    def activate(gate, up):
        return (gate / (1.0 + jnp.exp(-gate)) * up).astype(jnp.bfloat16)

    if main:
        hidden[0, :, :main] = activate(acc[:, :main], acc[:, main : 2 * main])
    if tail:
        ends_of = acc[:, 2 * main :]
        hidden[0, :, main:] = activate(ends_of[:, :tail], ends_of[:, tail:])

    hidden_share = pltpu.make_async_remote_copy(
        src_ref=hidden.at[0], dst_ref=hidden.at[1],
        send_sem=s_send.at[1], recv_sem=s_recv.at[1], device_id=sibling, device_id_type=MESH,
    )
    hidden_share.start()
    wd_load.wait()
    wd_share.wait_recv()
    hidden_share.wait_recv()

    scatter = {}

    def product(n, s):
        return jnp.dot(hidden[n], wd[n, :, cols(s)], preferred_element_type=jnp.float32)

    def scatter_send(s, n, src, dst, target):
        scatter[s, n] = send(src, dst, r_send, r_recv, s * 7 + n, target)

    def add_cores(s):
        chip_sum[:, :, :, cols(s)] = (
            (product(0, s) + product(1, s)).astype(jnp.bfloat16).reshape(SIDE, SIDE, CAP, pieces[s][1])
        )

    def start_big(s):
        c = cols(s)
        big, d = positions[s][1], forward[s]
        scatter_send(s, 1, quad_of(chip_sum, s, shift(big, 2)), big_in.at[0, :, :, c], on_big(s, d))
        scatter_send(s, 2, quad_of(chip_sum, s, shift(big, -d)), big_in.at[1, :, :, c], on_big(s, -d))

    def quad_load(s, big):
        c = cols(s)
        return (chip_sum[big, :, :, c] if turned(s) else chip_sum[:, big, :, c]).astype(jnp.float32)

    def add_relay(s):
        c = cols(s)
        big_in[0, :, :, c] = (
            quad_load(s, shift(positions[s][1], forward[s])) + big_in[0, :, :, c].astype(jnp.float32)
        ).astype(jnp.bfloat16)

    def relay(s):
        c = cols(s)
        scatter_send(s, 3, big_in.at[0, :, :, c], big_in.at[2, :, :, c], on_big(s, forward[s]))

    def add_quads(s):
        c = cols(s)
        quad_sum[:, :, c] = (
            quad_load(s, positions[s][1])
            + big_in[1, :, :, c].astype(jnp.float32)
            + big_in[2, :, :, c].astype(jnp.float32)
        ).astype(jnp.bfloat16)

    def start_small(s):
        c = cols(s)
        for by in range(1, SIDE):
            scatter_send(
                s, 3 + by, quad_sum.at[shift(positions[s][0], by), :, c],
                small_in.at[by - 1, :, c], on_small(s, by),
            )

    def add_blocks(s):
        c = cols(s)
        value = quad_sum[positions[s][0], :, c].astype(jnp.float32)
        for n in range(SIDE - 1):
            value = value + small_in[n, :, c].astype(jnp.float32)
        final[:, c] = value

    def step(waits, work, sends):
        for s, n in waits:
            scatter[s, n].wait_recv()
        for act, group in work:
            for s in group:
                act(s)
        for act, group in sends:
            for s in group:
                act(s)

    def came(group, *ns):
        return [(s, n) for s in group for n in ns]

    groups = [order[n : n + 2] for n in range(0, len(pieces), 2)]
    for n, group in enumerate(groups):
        step([], [(add_cores, group)], [(start_big, group)])
        if n == 3:
            step(came(groups[0], 1), [(add_relay, groups[0])], [(relay, groups[0])])
    for group in groups[1:]:
        step(came(group, 1), [(add_relay, group)], [(relay, group)])
    for group in groups:
        step(came(group, 2, 3), [(add_quads, group)], [(start_small, group)])
    for group in groups:
        step(came(group, 4, 5, 6), [(add_blocks, group)], [])

    for m in range(hb):
        spread2[pl.ds(m, CAP, stride=rp), :] = final[:, m * LANES : (m + 1) * LANES]
    for k in range(ROWS // CHIPS):
        rows_out[k] = spread2[k * rp : (k + 1) * rp, :].astype(jnp.bfloat16)
    for i in range(DEVICES):
        rank = offs[i] + row_for(chip, offs[i])
        pkt_back[i] = rows_out[jnp.minimum(rank // CHIPS, ROWS // CHIPS - 1)]
    inbox_back[me] = pkt_back[me]

    returned = exchange(lambda p, c: pkt_back.at[2 * p + c], inbox_back, b_send, b_recv)

    for copy in [wd_share, hidden_share] + dispatched + list(gather.values()) + list(scatter.values()):
        copy.wait_send()
    arrived(inbox_back, b_send, b_recv)

    for j in range(CAP):
        p = lax.rem(my_off + j, CHIPS)
        for h in range(2):
            row = inbox_back[2 * p + h].astype(jnp.float32)
            row = jnp.where(j < my_count, row, jnp.zeros_like(row))
            spread[(2 * j + h) * rp : (2 * j + h + 1) * rp, :] = row
    for h in range(2):
        for m in range(hb):
            block = spread[pl.ds(h * rp + m, CAP, stride=2 * rp), :]
            at = (h * hb + m) * LANES
            out[:, at : at + LANES] = block.astype(jnp.bfloat16)
    for copy in returned:
        copy.wait_send()


def local(requests, counts, gate_weight, up_weight, down_weight):
    capacity, features = requests.shape
    ff = gate_weight.shape[1]
    half = features // 2
    n_pieces = len(column_pieces(half))
    rp = -(-(half // LANES) // 16) * 16
    bf16, f32 = jnp.bfloat16, jnp.float32
    dma = pltpu.SemaphoreType.DMA
    return pl.pallas_call(
        kernel,
        out_shape=jax.ShapeDtypeStruct((capacity, features), bf16),
        in_specs=[
            pl.BlockSpec(memory_space=pl.ANY),
            pl.BlockSpec(memory_space=pltpu.SMEM),
            pl.BlockSpec(memory_space=pl.ANY),
            pl.BlockSpec(memory_space=pl.ANY),
            pl.BlockSpec(memory_space=pl.ANY),
        ],
        out_specs=pl.BlockSpec(memory_space=pltpu.VMEM),
        scratch_shapes=[
            pltpu.VMEM((capacity, features), bf16),
            pltpu.VMEM((2 * ff, features), bf16),
            pltpu.VMEM((2, ff, half), bf16),
            pltpu.VMEM((CAP * 2 * rp, LANES), f32),
            pltpu.VMEM((CAP * rp, LANES), f32),
            pltpu.VMEM((CHIPS, 2, rp, LANES), bf16),
            pltpu.VMEM((CAP, 2, rp, LANES), bf16),
            pltpu.VMEM((DEVICES, rp, LANES), bf16),
            pltpu.VMEM((2, SIDE, SIDE, CAP, half), bf16),
            pltpu.VMEM((ROWS, 2 * ff), f32),
            pltpu.VMEM((2, ROWS, ff), bf16),
            pltpu.VMEM((SIDE, SIDE, CAP, half), bf16),
            pltpu.VMEM((3, SIDE, CAP, half), bf16),
            pltpu.VMEM((SIDE, CAP, half), bf16),
            pltpu.VMEM((3, CAP, half), bf16),
            pltpu.VMEM((CAP, half), f32),
            pltpu.VMEM((ROWS // CHIPS, rp, LANES), bf16),
            pltpu.VMEM((DEVICES, rp, LANES), bf16),
            pltpu.VMEM((DEVICES, rp, LANES), bf16),
            pltpu.SMEM((DEVICES,), jnp.int32),
            dma((6,)),
            dma((2,)),
            dma((2,)),
            dma((DEVICES,)),
            dma((DEVICES,)),
            dma((n_pieces * 10,)),
            dma((n_pieces * 10,)),
            dma((n_pieces * 7,)),
            dma((n_pieces * 7,)),
            dma((DEVICES,)),
            dma((DEVICES,)),
        ],
        compiler_params=pltpu.CompilerParams(
            collective_id=0, has_side_effects=True, vmem_limit_bytes=58 * 2**20
        ),
        cost_estimate=pl.CostEstimate(
            flops=6 * ROWS * features * ff, bytes_accessed=6 * features * ff, transcendentals=ROWS * ff
        ),
        name="ffn",
    )(requests, counts, gate_weight.T, up_weight.T, down_weight)


def solution(mesh):
    return jax.shard_map(
        local,
        mesh=mesh,
        in_specs=(
            P(("group", "tensor"), None),
            P("group"),
            P(None, "tensor"),
            P(None, "tensor"),
            P("tensor", None),
        ),
        out_specs=P(("group", "tensor"), None),
        check_vma=False,
    )
```

```python
import functools

import jax
import jax.numpy as jnp
from jax import lax
from jax.experimental import pallas as pl
from jax.experimental.pallas import tpu as pltpu
from jax.sharding import PartitionSpec as P

SIDE = 4
CHIPS = SIDE * SIDE
DEVICES = 2 * CHIPS
CAP = 16
ROWS = 256
LANES = 128
MESH = pl.DeviceIdType.MESH


def column_pieces(half):
    tile = 256 if half % 512 == 0 and half >= 1024 else 128
    per_order = half // tile // 2
    pieces = []
    for n in range((per_order + 1) // 2):
        for turned in range(2):
            at = (turned * per_order + 2 * n) * tile
            pieces.append((at, min(2, per_order - 2 * n) * tile, turned, n % 2))
    return pieces


def kernel(
    req_hbm, counts, wgt_hbm, wut_hbm, wd_hbm, out,
    req, wgu, wd, spread, spread2, pkt, rows_in, inbox, grid, acc, hidden,
    chip_sum, big_in, quad_sum, small_in, final, rows_out, pkt_back, inbox_back, offs,
    w_sem, s_send, s_recv, a_send, a_recv, g_send, g_recv, r_send, r_recv, b_send, b_recv,
):
    features = req.shape[1]
    half = features // 2
    hb = half // LANES
    rp = inbox.shape[1]
    pieces = column_pieces(half)
    order = range(len(pieces))
    ff = wd.shape[1]
    main = ff // LANES * LANES
    tail = ff - main

    me = lax.axis_index("tensor")
    core = lax.rem(me, 2)
    other = 1 - core
    chip = me // 2
    x = chip // SIDE
    z = lax.rem(chip, SIDE)

    def device(xx, zz, cc):
        return {"tensor": (xx * SIDE + zz) * 2 + cc}

    sibling = device(x, z, other)

    def exchange(source, box, sends, recvs):
        copies = []
        for n, o in enumerate(others):
            to_chip, to_core = at_offset(o, 1)
            copy = pltpu.make_async_remote_copy(
                src_ref=source(to_chip, to_core), dst_ref=box.at[me],
                send_sem=sends.at[n], recv_sem=recvs.at[me],
                device_id={"tensor": 2 * to_chip + to_core}, device_id_type=MESH,
            )
            copy.start()
            copies.append(copy)
        return copies

    def arrived(box, sends, recvs):
        for n, o in enumerate(others):
            from_chip, from_core = at_offset(o, -1)
            origin = 2 * from_chip + from_core
            pltpu.make_async_remote_copy(
                src_ref=box.at[me], dst_ref=box.at[origin],
                send_sem=sends.at[n], recv_sem=recvs.at[origin],
                device_id={"tensor": origin}, device_id_type=MESH,
            ).wait_recv()

    hops = (0, 1, 2, 1)
    others = sorted(
        ((dx, dz, dc) for dx in range(SIDE) for dz in range(SIDE) for dc in range(2) if dx or dz or dc),
        key=lambda o: -hops[o[0]] - hops[o[1]],
    )

    def at_offset(o, sign):
        xx = lax.rem(x + sign * o[0] + SIDE, SIDE)
        zz = lax.rem(z + sign * o[1] + SIDE, SIDE)
        return xx * SIDE + zz, lax.rem(core + o[2], 2)

    req_load = pltpu.make_async_copy(req_hbm, req, w_sem.at[5])
    req_load.start()

    barrier = pltpu.get_barrier_semaphore()

    for o in others:
        to_chip, to_core = at_offset(o, 1)
        pl.semaphore_signal(
            barrier, inc=1, device_id={"tensor": 2 * to_chip + to_core}, device_id_type=MESH
        )

    loads = []
    for n, (src, at, size, to) in enumerate((
        (wgt_hbm, 0, main, 0),
        (wut_hbm, 0, main, main),
        (wgt_hbm, main, tail, 2 * main),
        (wut_hbm, main, tail, 2 * main + tail),
    )):
        if size:
            loads.append(
                pltpu.make_async_copy(src.at[pl.ds(at, size)], wgu.at[pl.ds(to, size)], w_sem.at[n])
            )
            loads[-1].start()
    wd_load = pltpu.make_async_copy(
        wd_hbm.at[:, pl.ds(pl.multiple_of(core * half, LANES), half)], wd.at[0], w_sem.at[4]
    )
    wd_load.start()

    total = jnp.int32(0)
    ends = []
    for i in range(DEVICES):
        offs[i] = total
        total = total + counts[i]
        ends.append(total)
    my_off = offs[me]
    my_count = counts[me]

    spread[...] = jnp.zeros_like(spread)
    req_load.wait()
    for h in range(2):
        for m in range(hb):
            block = req[:, (h * hb + m) * LANES : (h * hb + m + 1) * LANES]
            spread[pl.ds(h * rp + m, CAP, stride=2 * rp), :] = block.astype(jnp.float32)

    def row_for(p, off):
        return lax.rem(p - off + ROWS, CAP)

    for j in range(CAP):
        for h in range(2):
            at = (2 * j + h) * rp
            rows_in[j, h] = spread[at : at + rp, :].astype(jnp.bfloat16)
    for p in range(CHIPS):
        pkt[p] = rows_in[row_for(p, my_off)]
    inbox[me] = pkt[chip, core]

    pl.semaphore_wait(barrier, DEVICES - 1)

    wd_share = pltpu.make_async_remote_copy(
        src_ref=wd_hbm.at[:, pl.ds(pl.multiple_of(other * half, LANES), half)], dst_ref=wd.at[1],
        send_sem=s_send.at[0], recv_sem=s_recv.at[0], device_id=sibling, device_id_type=MESH,
    )
    dispatched = exchange(lambda p, c: pkt.at[p, c], inbox, a_send, a_recv)

    wd_share.start()

    owners = []
    for k in range(ROWS // CHIPS):
        rank = chip + CHIPS * k
        owner = jnp.int32(0)
        for end in ends[:-1]:
            owner = owner + (end <= rank).astype(jnp.int32)
        owners.append(owner)

    arrived(inbox, a_send, a_recv)

    for k in range(ROWS // CHIPS):
        spread2[k * rp : (k + 1) * rp, :] = inbox[owners[k]].astype(jnp.float32)
    for m in range(hb):
        block = spread2[pl.ds(m, CAP, stride=rp), :].astype(jnp.bfloat16)
        grid[core, x, z, :, m * LANES : (m + 1) * LANES] = block

    def cols(s):
        return pl.ds(pieces[s][0], pieces[s][1])

    def turned(s):
        return pieces[s][2]

    def quad_of(buf, s, big):
        return buf.at[big, :, :, cols(s)] if turned(s) else buf.at[:, big, :, cols(s)]

    positions = [(z, x) if turned(s) else (x, z) for s in order]
    forward = [(1 - 2 * pieces[s][3]) * (1 - 2 * core) for s in order]

    def shift(pos, by):
        return lax.rem(pos + by + 2 * SIDE, SIDE)

    def on_small(s, by):
        return device(x, shift(z, by), core) if turned(s) else device(shift(x, by), z, core)

    def on_big(s, by):
        return device(shift(x, by), z, core) if turned(s) else device(x, shift(z, by), core)

    def send(src, dst, sends, recvs, index, target):
        copy = pltpu.make_async_remote_copy(
            src_ref=src, dst_ref=dst, send_sem=sends.at[index], recv_sem=recvs.at[index],
            device_id=target, device_id_type=MESH,
        )
        copy.start()
        return copy

    gather = {}

    def gather_quad(s, n, big, target):
        ref = quad_of(grid.at[core], s, big)
        gather[s, n] = send(ref, ref, g_send, g_recv, s * 10 + n, target)

    for s in order:
        ref = grid.at[core, x, z, :, cols(s)]
        for by in range(1, SIDE):
            gather[s, by - 1] = send(ref, ref, g_send, g_recv, s * 10 + by - 1, on_small(s, by))
    for s in order:
        big = positions[s][1]
        for n in range(3):
            gather[s, n].wait_recv()
        gather_quad(s, 3, big, on_big(s, forward[s]))
        gather_quad(s, 4, big, on_big(s, -forward[s]))
        gather_quad(s, 6, big, sibling)
    for s in order:
        behind = shift(positions[s][1], -forward[s])
        gather[s, 3].wait_recv()
        gather_quad(s, 5, behind, on_big(s, forward[s]))
        gather_quad(s, 7, behind, sibling)

    for copy in loads:
        copy.wait()

    def contract(c, s):
        at, width = pieces[s][:2]
        col = pl.ds(pl.multiple_of(c * half + at, LANES), width)
        lhs = grid[c, :, :, :, at : at + width].reshape(ROWS, width)
        return lax.dot_general(
            lhs, wgu[:, col], (((1,), (1,)), ((), ())), preferred_element_type=jnp.float32
        )

    def arrive(s):
        big = positions[s][1]
        gather[s, 4].wait_recv()
        gather_quad(s, 8, shift(big, forward[s]), sibling)
        gather[s, 5].wait_recv()
        gather_quad(s, 9, shift(big, 2), sibling)

    def from_sibling(s):
        for n in (6, 7, 8, 9):
            gather[s, n].wait_recv()

    first, second = order[: len(pieces) // 2], order[len(pieces) // 2 :]
    for s in first:
        arrive(s)
    acc[...] = sum(contract(core, s) for s in first)
    for s in second:
        arrive(s)
    for s in first:
        from_sibling(s)
    acc[...] += sum([contract(core, s) for s in second] + [contract(other, s) for s in first])
    for s in second:
        from_sibling(s)
    acc[...] += sum(contract(other, s) for s in second)

    def activate(gate, up):
        return (gate / (1.0 + jnp.exp(-gate)) * up).astype(jnp.bfloat16)

    if main:
        hidden[0, :, :main] = activate(acc[:, :main], acc[:, main : 2 * main])
    if tail:
        ends_of = acc[:, 2 * main :]
        hidden[0, :, main:] = activate(ends_of[:, :tail], ends_of[:, tail:])

    hidden_share = pltpu.make_async_remote_copy(
        src_ref=hidden.at[0], dst_ref=hidden.at[1],
        send_sem=s_send.at[1], recv_sem=s_recv.at[1], device_id=sibling, device_id_type=MESH,
    )
    hidden_share.start()
    wd_load.wait()
    wd_share.wait_recv()
    hidden_share.wait_recv()

    scatter = {}

    def product(n, s):
        return jnp.dot(hidden[n], wd[n, :, cols(s)], preferred_element_type=jnp.float32)

    def scatter_send(s, n, src, dst, target):
        scatter[s, n] = send(src, dst, r_send, r_recv, s * 7 + n, target)

    def add_cores(s):
        chip_sum[:, :, :, cols(s)] = (
            (product(0, s) + product(1, s)).astype(jnp.bfloat16).reshape(SIDE, SIDE, CAP, pieces[s][1])
        )

    def start_big(s):
        c = cols(s)
        big, d = positions[s][1], forward[s]
        scatter_send(s, 1, quad_of(chip_sum, s, shift(big, 2)), big_in.at[0, :, :, c], on_big(s, d))
        scatter_send(s, 2, quad_of(chip_sum, s, shift(big, -d)), big_in.at[1, :, :, c], on_big(s, -d))

    def quad_load(s, big):
        c = cols(s)
        return (chip_sum[big, :, :, c] if turned(s) else chip_sum[:, big, :, c]).astype(jnp.float32)

    def add_relay(s):
        c = cols(s)
        big_in[0, :, :, c] = (
            quad_load(s, shift(positions[s][1], forward[s])) + big_in[0, :, :, c].astype(jnp.float32)
        ).astype(jnp.bfloat16)

    def relay(s):
        c = cols(s)
        scatter_send(s, 3, big_in.at[0, :, :, c], big_in.at[2, :, :, c], on_big(s, forward[s]))

    def add_quads(s):
        c = cols(s)
        quad_sum[:, :, c] = (
            quad_load(s, positions[s][1])
            + big_in[1, :, :, c].astype(jnp.float32)
            + big_in[2, :, :, c].astype(jnp.float32)
        ).astype(jnp.bfloat16)

    def start_small(s):
        c = cols(s)
        for by in range(1, SIDE):
            scatter_send(
                s, 3 + by, quad_sum.at[shift(positions[s][0], by), :, c],
                small_in.at[by - 1, :, c], on_small(s, by),
            )

    def add_blocks(s):
        c = cols(s)
        value = quad_sum[positions[s][0], :, c].astype(jnp.float32)
        for n in range(SIDE - 1):
            value = value + small_in[n, :, c].astype(jnp.float32)
        final[:, c] = value

    def step(waits, work, sends):
        for s, n in waits:
            scatter[s, n].wait_recv()
        for act, group in work:
            for s in group:
                act(s)
        for act, group in sends:
            for s in group:
                act(s)

    def came(group, *ns):
        return [(s, n) for s in group for n in ns]

    groups = [order[n : n + 2] for n in range(0, len(pieces), 2)]
    for n, group in enumerate(groups):
        step([], [(add_cores, group)], [(start_big, group)])
        if n == 3:
            step(came(groups[0], 1), [(add_relay, groups[0])], [(relay, groups[0])])
    for group in groups[1:]:
        step(came(group, 1), [(add_relay, group)], [(relay, group)])
    for group in groups:
        step(came(group, 2, 3), [(add_quads, group)], [(start_small, group)])
    for group in groups:
        step(came(group, 4, 5, 6), [(add_blocks, group)], [])

    for m in range(hb):
        spread2[pl.ds(m, CAP, stride=rp), :] = final[:, m * LANES : (m + 1) * LANES]
    for k in range(ROWS // CHIPS):
        rows_out[k] = spread2[k * rp : (k + 1) * rp, :].astype(jnp.bfloat16)
    for i in range(DEVICES):
        rank = offs[i] + row_for(chip, offs[i])
        pkt_back[i] = rows_out[jnp.minimum(rank // CHIPS, ROWS // CHIPS - 1)]
    inbox_back[me] = pkt_back[me]

    returned = exchange(lambda p, c: pkt_back.at[2 * p + c], inbox_back, b_send, b_recv)

    for copy in [wd_share, hidden_share] + dispatched + list(gather.values()) + list(scatter.values()):
        copy.wait_send()
    arrived(inbox_back, b_send, b_recv)

    for j in range(CAP):
        p = lax.rem(my_off + j, CHIPS)
        for h in range(2):
            row = inbox_back[2 * p + h].astype(jnp.float32)
            row = jnp.where(j < my_count, row, jnp.zeros_like(row))
            spread[(2 * j + h) * rp : (2 * j + h + 1) * rp, :] = row
    for h in range(2):
        for m in range(hb):
            block = spread[pl.ds(h * rp + m, CAP, stride=2 * rp), :]
            at = (h * hb + m) * LANES
            out[:, at : at + LANES] = block.astype(jnp.bfloat16)
    for copy in returned:
        copy.wait_send()


def local(requests, counts, gate_weight, up_weight, down_weight):
    capacity, features = requests.shape
    ff = gate_weight.shape[1]
    half = features // 2
    n_pieces = len(column_pieces(half))
    rp = -(-(half // LANES) // 16) * 16
    bf16, f32 = jnp.bfloat16, jnp.float32
    dma = pltpu.SemaphoreType.DMA
    return pl.pallas_call(
        kernel,
        out_shape=jax.ShapeDtypeStruct((capacity, features), bf16),
        in_specs=[
            pl.BlockSpec(memory_space=pl.ANY),
            pl.BlockSpec(memory_space=pltpu.SMEM),
            pl.BlockSpec(memory_space=pl.ANY),
            pl.BlockSpec(memory_space=pl.ANY),
            pl.BlockSpec(memory_space=pl.ANY),
        ],
        out_specs=pl.BlockSpec(memory_space=pltpu.VMEM),
        scratch_shapes=[
            pltpu.VMEM((capacity, features), bf16),
            pltpu.VMEM((2 * ff, features), bf16),
            pltpu.VMEM((2, ff, half), bf16),
            pltpu.VMEM((CAP * 2 * rp, LANES), f32),
            pltpu.VMEM((CAP * rp, LANES), f32),
            pltpu.VMEM((CHIPS, 2, rp, LANES), bf16),
            pltpu.VMEM((CAP, 2, rp, LANES), bf16),
            pltpu.VMEM((DEVICES, rp, LANES), bf16),
            pltpu.VMEM((2, SIDE, SIDE, CAP, half), bf16),
            pltpu.VMEM((ROWS, 2 * ff), f32),
            pltpu.VMEM((2, ROWS, ff), bf16),
            pltpu.VMEM((SIDE, SIDE, CAP, half), bf16),
            pltpu.VMEM((3, SIDE, CAP, half), bf16),
            pltpu.VMEM((SIDE, CAP, half), bf16),
            pltpu.VMEM((3, CAP, half), bf16),
            pltpu.VMEM((CAP, half), f32),
            pltpu.VMEM((ROWS // CHIPS, rp, LANES), bf16),
            pltpu.VMEM((DEVICES, rp, LANES), bf16),
            pltpu.VMEM((DEVICES, rp, LANES), bf16),
            pltpu.SMEM((DEVICES,), jnp.int32),
            dma((6,)),
            dma((2,)),
            dma((2,)),
            dma((DEVICES,)),
            dma((DEVICES,)),
            dma((n_pieces * 10,)),
            dma((n_pieces * 10,)),
            dma((n_pieces * 7,)),
            dma((n_pieces * 7,)),
            dma((DEVICES,)),
            dma((DEVICES,)),
        ],
        compiler_params=pltpu.CompilerParams(
            collective_id=0, has_side_effects=True, vmem_limit_bytes=58 * 2**20
        ),
        cost_estimate=pl.CostEstimate(
            flops=6 * ROWS * features * ff, bytes_accessed=6 * features * ff, transcendentals=ROWS * ff
        ),
        name="ffn",
    )(requests, counts, gate_weight.T, up_weight.T, down_weight)


def solution(mesh):
    return jax.shard_map(
        local,
        mesh=mesh,
        in_specs=(
            P(("group", "tensor"), None),
            P("group"),
            P(None, "tensor"),
            P(None, "tensor"),
            P("tensor", None),
        ),
        out_specs=P(("group", "tensor"), None),
        check_vma=False,
    )
```

```python
import functools

import jax
import jax.numpy as jnp
from jax import lax
from jax.experimental import pallas as pl
from jax.experimental.pallas import tpu as pltpu
from jax.sharding import PartitionSpec as P

SIDE = 4
CHIPS = SIDE * SIDE
DEVICES = 2 * CHIPS
CAP = 16
ROWS = 256
LANES = 128
MESH = pl.DeviceIdType.MESH


def column_pieces(half):
    tile = 256 if half % 512 == 0 and half >= 1024 else 128
    per_order = half // tile // 2
    pieces = []
    for n in range((per_order + 1) // 2):
        for turned in range(2):
            at = (turned * per_order + 2 * n) * tile
            pieces.append((at, min(2, per_order - 2 * n) * tile, turned, n % 2))
    return pieces


def kernel(
    req_hbm, counts, wgt_hbm, wut_hbm, wd_hbm, out,
    req, wgu, wd, spread, spread2, pkt, rows_in, inbox, grid, acc, hidden,
    chip_sum, big_in, quad_sum, small_in, final, rows_out, pkt_back, inbox_back, offs,
    w_sem, s_send, s_recv, a_send, a_recv, g_send, g_recv, r_send, r_recv, b_send, b_recv,
):
    features = req.shape[1]
    half = features // 2
    hb = half // LANES
    rp = inbox.shape[1]
    pieces = column_pieces(half)
    order = range(len(pieces))
    ff = wd.shape[1]
    main = ff // LANES * LANES
    tail = ff - main

    me = lax.axis_index("tensor")
    core = lax.rem(me, 2)
    other = 1 - core
    chip = me // 2
    x = chip // SIDE
    z = lax.rem(chip, SIDE)

    def device(xx, zz, cc):
        return {"tensor": (xx * SIDE + zz) * 2 + cc}

    sibling = device(x, z, other)

    def exchange(source, box, sends, recvs):
        copies = []
        for n, o in enumerate(others):
            to_chip, to_core = at_offset(o, 1)
            copy = pltpu.make_async_remote_copy(
                src_ref=source(to_chip, to_core), dst_ref=box.at[me],
                send_sem=sends.at[n], recv_sem=recvs.at[me],
                device_id={"tensor": 2 * to_chip + to_core}, device_id_type=MESH,
            )
            copy.start()
            copies.append(copy)
        return copies

    def arrived(box, sends, recvs):
        for n, o in enumerate(others):
            from_chip, from_core = at_offset(o, -1)
            origin = 2 * from_chip + from_core
            pltpu.make_async_remote_copy(
                src_ref=box.at[me], dst_ref=box.at[origin],
                send_sem=sends.at[n], recv_sem=recvs.at[origin],
                device_id={"tensor": origin}, device_id_type=MESH,
            ).wait_recv()

    hops = (0, 1, 2, 1)
    others = sorted(
        ((dx, dz, dc) for dx in range(SIDE) for dz in range(SIDE) for dc in range(2) if dx or dz or dc),
        key=lambda o: -hops[o[0]] - hops[o[1]],
    )

    def at_offset(o, sign):
        xx = lax.rem(x + sign * o[0] + SIDE, SIDE)
        zz = lax.rem(z + sign * o[1] + SIDE, SIDE)
        return xx * SIDE + zz, lax.rem(core + o[2], 2)

    req_load = pltpu.make_async_copy(req_hbm, req, w_sem.at[5])
    req_load.start()

    barrier = pltpu.get_barrier_semaphore()

    for o in others:
        to_chip, to_core = at_offset(o, 1)
        pl.semaphore_signal(
            barrier, inc=1, device_id={"tensor": 2 * to_chip + to_core}, device_id_type=MESH
        )

    loads = []
    for n, (src, at, size, to) in enumerate((
        (wgt_hbm, 0, main, 0),
        (wut_hbm, 0, main, main),
        (wgt_hbm, main, tail, 2 * main),
        (wut_hbm, main, tail, 2 * main + tail),
    )):
        if size:
            loads.append(
                pltpu.make_async_copy(src.at[pl.ds(at, size)], wgu.at[pl.ds(to, size)], w_sem.at[n])
            )
            loads[-1].start()
    wd_load = pltpu.make_async_copy(
        wd_hbm.at[:, pl.ds(pl.multiple_of(core * half, LANES), half)], wd.at[0], w_sem.at[4]
    )
    wd_load.start()

    total = jnp.int32(0)
    ends = []
    for i in range(DEVICES):
        offs[i] = total
        total = total + counts[i]
        ends.append(total)
    my_off = offs[me]
    my_count = counts[me]

    spread[...] = jnp.zeros_like(spread)
    req_load.wait()
    for h in range(2):
        for m in range(hb):
            block = req[:, (h * hb + m) * LANES : (h * hb + m + 1) * LANES]
            spread[pl.ds(h * rp + m, CAP, stride=2 * rp), :] = block.astype(jnp.float32)

    def row_for(p, off):
        return lax.rem(p - off + ROWS, CAP)

    for j in range(CAP):
        for h in range(2):
            at = (2 * j + h) * rp
            rows_in[j, h] = spread[at : at + rp, :].astype(jnp.bfloat16)
    for p in range(CHIPS):
        pkt[p] = rows_in[row_for(p, my_off)]
    inbox[me] = pkt[chip, core]

    pl.semaphore_wait(barrier, DEVICES - 1)

    wd_share = pltpu.make_async_remote_copy(
        src_ref=wd_hbm.at[:, pl.ds(pl.multiple_of(other * half, LANES), half)], dst_ref=wd.at[1],
        send_sem=s_send.at[0], recv_sem=s_recv.at[0], device_id=sibling, device_id_type=MESH,
    )
    dispatched = exchange(lambda p, c: pkt.at[p, c], inbox, a_send, a_recv)

    wd_share.start()

    owners = []
    for k in range(ROWS // CHIPS):
        rank = chip + CHIPS * k
        owner = jnp.int32(0)
        for end in ends[:-1]:
            owner = owner + (end <= rank).astype(jnp.int32)
        owners.append(owner)

    arrived(inbox, a_send, a_recv)

    for k in range(ROWS // CHIPS):
        spread2[k * rp : (k + 1) * rp, :] = inbox[owners[k]].astype(jnp.float32)
    for m in range(hb):
        block = spread2[pl.ds(m, CAP, stride=rp), :].astype(jnp.bfloat16)
        grid[core, x, z, :, m * LANES : (m + 1) * LANES] = block

    def cols(s):
        return pl.ds(pieces[s][0], pieces[s][1])

    def turned(s):
        return pieces[s][2]

    def quad_of(buf, s, big):
        return buf.at[big, :, :, cols(s)] if turned(s) else buf.at[:, big, :, cols(s)]

    positions = [(z, x) if turned(s) else (x, z) for s in order]
    forward = [(1 - 2 * pieces[s][3]) * (1 - 2 * core) for s in order]

    def shift(pos, by):
        return lax.rem(pos + by + 2 * SIDE, SIDE)

    def on_small(s, by):
        return device(x, shift(z, by), core) if turned(s) else device(shift(x, by), z, core)

    def on_big(s, by):
        return device(shift(x, by), z, core) if turned(s) else device(x, shift(z, by), core)

    def send(src, dst, sends, recvs, index, target):
        copy = pltpu.make_async_remote_copy(
            src_ref=src, dst_ref=dst, send_sem=sends.at[index], recv_sem=recvs.at[index],
            device_id=target, device_id_type=MESH,
        )
        copy.start()
        return copy

    gather = {}

    def gather_quad(s, n, big, target):
        ref = quad_of(grid.at[core], s, big)
        gather[s, n] = send(ref, ref, g_send, g_recv, s * 10 + n, target)

    for s in order:
        ref = grid.at[core, x, z, :, cols(s)]
        for by in range(1, SIDE):
            gather[s, by - 1] = send(ref, ref, g_send, g_recv, s * 10 + by - 1, on_small(s, by))
    for s in order:
        big = positions[s][1]
        for n in range(3):
            gather[s, n].wait_recv()
        gather_quad(s, 3, big, on_big(s, forward[s]))
        gather_quad(s, 4, big, on_big(s, -forward[s]))
        gather_quad(s, 6, big, sibling)
    for s in order:
        behind = shift(positions[s][1], -forward[s])
        gather[s, 3].wait_recv()
        gather_quad(s, 5, behind, on_big(s, forward[s]))
        gather_quad(s, 7, behind, sibling)

    for copy in loads:
        copy.wait()

    def contract(c, s):
        at, width = pieces[s][:2]
        col = pl.ds(pl.multiple_of(c * half + at, LANES), width)
        lhs = grid[c, :, :, :, at : at + width].reshape(ROWS, width)
        return lax.dot_general(
            lhs, wgu[:, col], (((1,), (1,)), ((), ())), preferred_element_type=jnp.float32
        )

    def arrive(s):
        big = positions[s][1]
        gather[s, 4].wait_recv()
        gather_quad(s, 8, shift(big, forward[s]), sibling)
        gather[s, 5].wait_recv()
        gather_quad(s, 9, shift(big, 2), sibling)

    def from_sibling(s):
        for n in (6, 7, 8, 9):
            gather[s, n].wait_recv()

    first, second = order[: len(pieces) // 2], order[len(pieces) // 2 :]
    for s in first:
        arrive(s)
    acc[...] = sum(contract(core, s) for s in first)
    for s in second:
        arrive(s)
    for s in first:
        from_sibling(s)
    acc[...] += sum([contract(core, s) for s in second] + [contract(other, s) for s in first])
    for s in second:
        from_sibling(s)
    acc[...] += sum(contract(other, s) for s in second)

    def activate(gate, up):
        return (gate / (1.0 + jnp.exp(-gate)) * up).astype(jnp.bfloat16)

    if main:
        hidden[0, :, :main] = activate(acc[:, :main], acc[:, main : 2 * main])
    if tail:
        ends_of = acc[:, 2 * main :]
        hidden[0, :, main:] = activate(ends_of[:, :tail], ends_of[:, tail:])

    hidden_share = pltpu.make_async_remote_copy(
        src_ref=hidden.at[0], dst_ref=hidden.at[1],
        send_sem=s_send.at[1], recv_sem=s_recv.at[1], device_id=sibling, device_id_type=MESH,
    )
    hidden_share.start()
    wd_load.wait()
    wd_share.wait_recv()
    hidden_share.wait_recv()

    scatter = {}

    def product(n, s):
        return jnp.dot(hidden[n], wd[n, :, cols(s)], preferred_element_type=jnp.float32)

    def scatter_send(s, n, src, dst, target):
        scatter[s, n] = send(src, dst, r_send, r_recv, s * 7 + n, target)

    def add_cores(s):
        chip_sum[:, :, :, cols(s)] = (
            (product(0, s) + product(1, s)).astype(jnp.bfloat16).reshape(SIDE, SIDE, CAP, pieces[s][1])
        )

    def start_big(s):
        c = cols(s)
        big, d = positions[s][1], forward[s]
        scatter_send(s, 1, quad_of(chip_sum, s, shift(big, 2)), big_in.at[0, :, :, c], on_big(s, d))
        scatter_send(s, 2, quad_of(chip_sum, s, shift(big, -d)), big_in.at[1, :, :, c], on_big(s, -d))

    def quad_load(s, big):
        c = cols(s)
        return (chip_sum[big, :, :, c] if turned(s) else chip_sum[:, big, :, c]).astype(jnp.float32)

    def add_relay(s):
        c = cols(s)
        big_in[0, :, :, c] = (
            quad_load(s, shift(positions[s][1], forward[s])) + big_in[0, :, :, c].astype(jnp.float32)
        ).astype(jnp.bfloat16)

    def relay(s):
        c = cols(s)
        scatter_send(s, 3, big_in.at[0, :, :, c], big_in.at[2, :, :, c], on_big(s, forward[s]))

    def add_quads(s):
        c = cols(s)
        quad_sum[:, :, c] = (
            quad_load(s, positions[s][1])
            + big_in[1, :, :, c].astype(jnp.float32)
            + big_in[2, :, :, c].astype(jnp.float32)
        ).astype(jnp.bfloat16)

    def start_small(s):
        c = cols(s)
        for by in range(1, SIDE):
            scatter_send(
                s, 3 + by, quad_sum.at[shift(positions[s][0], by), :, c],
                small_in.at[by - 1, :, c], on_small(s, by),
            )

    def add_blocks(s):
        c = cols(s)
        value = quad_sum[positions[s][0], :, c].astype(jnp.float32)
        for n in range(SIDE - 1):
            value = value + small_in[n, :, c].astype(jnp.float32)
        final[:, c] = value

    def step(waits, work, sends):
        for s, n in waits:
            scatter[s, n].wait_recv()
        for act, group in work:
            for s in group:
                act(s)
        for act, group in sends:
            for s in group:
                act(s)

    def came(group, *ns):
        return [(s, n) for s in group for n in ns]

    groups = [order[n : n + 2] for n in range(0, len(pieces), 2)]
    for n, group in enumerate(groups):
        step([], [(add_cores, group)], [(start_big, group)])
        if n == 3:
            step(came(groups[0], 1), [(add_relay, groups[0])], [(relay, groups[0])])
    for group in groups[1:]:
        step(came(group, 1), [(add_relay, group)], [(relay, group)])
    for group in groups:
        step(came(group, 2, 3), [(add_quads, group)], [(start_small, group)])
    for group in groups:
        step(came(group, 4, 5, 6), [(add_blocks, group)], [])

    for m in range(hb):
        spread2[pl.ds(m, CAP, stride=rp), :] = final[:, m * LANES : (m + 1) * LANES]
    for k in range(ROWS // CHIPS):
        rows_out[k] = spread2[k * rp : (k + 1) * rp, :].astype(jnp.bfloat16)
    for i in range(DEVICES):
        rank = offs[i] + row_for(chip, offs[i])
        pkt_back[i] = rows_out[jnp.minimum(rank // CHIPS, ROWS // CHIPS - 1)]
    inbox_back[me] = pkt_back[me]

    returned = exchange(lambda p, c: pkt_back.at[2 * p + c], inbox_back, b_send, b_recv)

    for copy in [wd_share, hidden_share] + dispatched + list(gather.values()) + list(scatter.values()):
        copy.wait_send()
    arrived(inbox_back, b_send, b_recv)

    for j in range(CAP):
        p = lax.rem(my_off + j, CHIPS)
        for h in range(2):
            row = inbox_back[2 * p + h].astype(jnp.float32)
            row = jnp.where(j < my_count, row, jnp.zeros_like(row))
            spread[(2 * j + h) * rp : (2 * j + h + 1) * rp, :] = row
    for h in range(2):
        for m in range(hb):
            block = spread[pl.ds(h * rp + m, CAP, stride=2 * rp), :]
            at = (h * hb + m) * LANES
            out[:, at : at + LANES] = block.astype(jnp.bfloat16)
    for copy in returned:
        copy.wait_send()


def local(requests, counts, gate_weight, up_weight, down_weight):
    capacity, features = requests.shape
    ff = gate_weight.shape[1]
    half = features // 2
    n_pieces = len(column_pieces(half))
    rp = -(-(half // LANES) // 16) * 16
    bf16, f32 = jnp.bfloat16, jnp.float32
    dma = pltpu.SemaphoreType.DMA
    return pl.pallas_call(
        kernel,
        out_shape=jax.ShapeDtypeStruct((capacity, features), bf16),
        in_specs=[
            pl.BlockSpec(memory_space=pl.ANY),
            pl.BlockSpec(memory_space=pltpu.SMEM),
            pl.BlockSpec(memory_space=pl.ANY),
            pl.BlockSpec(memory_space=pl.ANY),
            pl.BlockSpec(memory_space=pl.ANY),
        ],
        out_specs=pl.BlockSpec(memory_space=pltpu.VMEM),
        scratch_shapes=[
            pltpu.VMEM((capacity, features), bf16),
            pltpu.VMEM((2 * ff, features), bf16),
            pltpu.VMEM((2, ff, half), bf16),
            pltpu.VMEM(((CAP + 1) * 2 * rp, LANES), f32),
            pltpu.VMEM(((CAP + 1) * rp, LANES), f32),
            pltpu.VMEM((CHIPS, 2, rp, LANES), bf16),
            pltpu.VMEM((CAP, 2, rp, LANES), bf16),
            pltpu.VMEM((DEVICES, rp, LANES), bf16),
            pltpu.VMEM((2, SIDE, SIDE, CAP, half), bf16),
            pltpu.VMEM((ROWS, 2 * ff), f32),
            pltpu.VMEM((2, ROWS, ff), bf16),
            pltpu.VMEM((SIDE, SIDE, CAP, half), bf16),
            pltpu.VMEM((3, SIDE, CAP, half), bf16),
            pltpu.VMEM((SIDE, CAP, half), bf16),
            pltpu.VMEM((3, CAP, half), bf16),
            pltpu.VMEM((CAP, half), f32),
            pltpu.VMEM((ROWS // CHIPS, rp, LANES), bf16),
            pltpu.VMEM((DEVICES, rp, LANES), bf16),
            pltpu.VMEM((DEVICES, rp, LANES), bf16),
            pltpu.SMEM((DEVICES,), jnp.int32),
            dma((6,)),
            dma((2,)),
            dma((2,)),
            dma((DEVICES,)),
            dma((DEVICES,)),
            dma((n_pieces * 10,)),
            dma((n_pieces * 10,)),
            dma((n_pieces * 7,)),
            dma((n_pieces * 7,)),
            dma((DEVICES,)),
            dma((DEVICES,)),
        ],
        compiler_params=pltpu.CompilerParams(
            collective_id=0, has_side_effects=True, vmem_limit_bytes=58 * 2**20
        ),
        cost_estimate=pl.CostEstimate(
            flops=6 * ROWS * features * ff, bytes_accessed=6 * features * ff, transcendentals=ROWS * ff
        ),
        name="ffn",
    )(requests, counts, gate_weight.T, up_weight.T, down_weight)


def solution(mesh):
    return jax.shard_map(
        local,
        mesh=mesh,
        in_specs=(
            P(("group", "tensor"), None),
            P("group"),
            P(None, "tensor"),
            P(None, "tensor"),
            P("tensor", None),
        ),
        out_specs=P(("group", "tensor"), None),
        check_vma=False,
    )
```
